512 devices in a mesh: ens: 16 (over x_lo, y), space: 32 (over x_hi, z, core).
Axes of the slice: x: 4 (x_hi: 2, x_lo: 2; x = x_hi * 2 + x_lo), y: 8, z: 8, core: 2. Of those that a mesh axis runs over, the one named last changes fastest.
Arguments:
- member_embedding: bfloat16 [16, 512, 32, 720], P('ens', None, 'space'), may hold values from -6 to 6
- weights: bfloat16 [9, 100, 512], replicated, may hold values from -0.09375 to 0.09375
- verifying_observed_grid: float32 [100, 32, 720], P(None, 'space', 'ens'), may hold values from -6 to 6
- area_weight: float32 [32], P('space'), may hold values from 0.3 to 3
Outputs:
- crps_objective: float32 [], replicated
- latent_derivative: bfloat16 [16, 512, 32, 720], P('ens', None, 'space')
- grad_weight: float32 [9, 100, 512], replicated
The draws below stay inside these ranges and needn't reach their ends.
All inputs are finite; a program needn't handle non-finite values.
Results may differ from the reference program's by a relative error of at most 0.0085.
Values may be sent and summed in bfloat16 or wider, within the bound.
A program may use at most 64 MiB of HBM per device.

```python
import math
import jax
import jax.numpy as jnp
from jax import lax

CH = 100
LATENT = 512
LON = 720
TAPS = 9
MEMBERS = 16
NLAT = 32


def block_levels(rng, shape, pieces, smallest, top_value):
    gain, own = 1.0, jax.random.fold_in(rng, 6)
    for dim, blocks in pieces:
        heights = jnp.exp(jax.random.uniform(jax.random.fold_in(own, dim), (blocks,), jnp.float32, smallest / len(pieces), top_value / len(pieces)))
        gain = gain * jnp.repeat(heights, shape[dim] // blocks).reshape([-1 if axis == dim else 1 for axis in range(len(shape))])
    return gain


def bell_draw(stream_key, shape, width, reach, shards=(), kind=jnp.bfloat16):
    entries = jax.random.normal(stream_key, shape, jnp.float32) * width
    if len(shards) > 0:
        entries = block_levels(stream_key, shape, shards, -0.22, 0.18) * entries
    return jnp.clip(entries, min=-reach, max=reach).astype(kind)


def setup_inputs(seed: int = 0) -> dict:
    splits = jax.random.split(jax.random.key(seed), 5)
    member_embedding = bell_draw(splits[0], (MEMBERS, LATENT, NLAT, LON), 1.0, 6.0, ((0, 16), (2, 32)))
    weights = bell_draw(splits[1], (TAPS, CH, LATENT), (TAPS * LATENT) ** -0.5, 0.09375)
    verifying_observed_grid = bell_draw(splits[2], (CH, NLAT, LON), 1.0, 6.0, ((1, 32), (2, 16)), jnp.float32)
    area_weight = jnp.clip(jnp.exp(math.log(3.0) - 2.3025851 * jax.random.uniform(splits[3], (NLAT,), jnp.float32) ** block_levels(splits[3], (NLAT,), ((0, 32),), -0.2, 0.2)), 0.3, 3.0)
    return {"member_embedding": member_embedding, "weights": weights, "verifying_observed_grid": verifying_observed_grid, "area_weight": area_weight}


smoothing = 0.01
fairness = 0.95

def tap_scale(row_values, grid_rows):
    latitude = math.pi * ((row_values.astype(jnp.float32) + 0.5) / grid_rows - 0.5)
    east_west = 1.0 / (0.25 + jnp.cos(latitude))
    plain = jnp.ones_like(east_west)
    scales = []
    for tap_index in range(9):
        row_off = tap_index // 3 - 1
        col_off = tap_index % 3 - 1
        scales.append(east_west if row_off == 0 and col_off != 0 else plain)
    return jnp.stack(scales)

def reference(member_embedding, weights, verifying_observed_grid, area_weight):
    members, internal_embedding, grid_rows, longitudes = member_embedding.shape
    feature_sequence = weights.shape[1]
    rows_index = jnp.arange(grid_rows, dtype=jnp.int32)
    scales = tap_scale(rows_index, grid_rows)

    def apply_readout_map(field):
        padded = jnp.pad(field, ((0, 0), (1, 1), (0, 0)))
        overall_accumulated = jnp.zeros((feature_sequence, grid_rows, longitudes), jnp.float32)
        for tap_index in range(9):
            row_off = tap_index // 3 - 1
            col_off = tap_index % 3 - 1
            source = jnp.roll(padded[:, 1 + row_off:1 + row_off + grid_rows, :], -col_off, axis=2)
            product = jnp.dot(weights[tap_index], source.reshape(internal_embedding, -1), preferred_element_type=jnp.float32)
            overall_accumulated = overall_accumulated + product.reshape(feature_sequence, grid_rows, longitudes) * scales[tap_index][None, :, None]
        return overall_accumulated.astype(jnp.bfloat16)
    outcome_grids = lax.map(apply_readout_map, member_embedding)
    epsilon = (1.0 - fairness) / members
    pair_coef = (1.0 - epsilon) / (members - 1)

    def spread_accuracy_metric(inputs):
        values, observed = inputs
        values = values.astype(jnp.float32)
        diff_obs = values - observed[None]
        root_obs = jnp.sqrt(diff_obs * diff_obs + smoothing)

        def add_member(member, totals):
            pair_grad, pair_sum = totals
            other = lax.dynamic_index_in_dim(values, member, 0, keepdims=False)
            delta = values - other[None]
            root = jnp.sqrt(delta * delta + smoothing)
            return (pair_grad + delta / root, pair_sum + lax.optimization_barrier(jnp.sum(root, axis=0)))
        empty_zeros = jnp.zeros_like(values)
        pair_grad, pair_sum = lax.fori_loop(0, members, add_member, (empty_zeros, empty_zeros[0]))
        crps = lax.optimization_barrier(jnp.sum(root_obs, axis=0)) - 0.5 * pair_coef * pair_sum
        loss_part = jnp.sum(area_weight[:, None] * crps)
        gradient = area_weight[None, :, None] * (diff_obs / root_obs - pair_coef * pair_grad)
        return (gradient.astype(jnp.bfloat16), loss_part)
    slope_wrt_input, segment_costs_table = lax.map(spread_accuracy_metric, (jnp.swapaxes(outcome_grids, 0, 1), verifying_observed_grid))
    prediction_derivative = jnp.swapaxes(slope_wrt_input, 0, 1)
    tally_number = members * grid_rows * longitudes
    crps_objective = jnp.sum(segment_costs_table) / tally_number

    def adjoint_sweep(weight_total, inputs):
        field, grad_field = inputs
        padded = jnp.pad(field, ((0, 0), (1, 1), (0, 0)))
        grad_pad = jnp.pad(grad_field, ((0, 0), (1, 1), (0, 0)))
        grad_total = jnp.zeros((internal_embedding, grid_rows, longitudes), jnp.float32)
        updates = []
        for tap_index in range(9):
            row_off = tap_index // 3 - 1
            col_off = tap_index % 3 - 1
            source = jnp.roll(padded[:, 1 + row_off:1 + row_off + grid_rows, :], -col_off, axis=2)
            outer = jnp.einsum('crl,krl->rck', grad_field.astype(jnp.float32), source.astype(jnp.float32))
            updates.append(lax.optimization_barrier(jnp.sum(outer * scales[tap_index][:, None, None], axis=0)))
            earlier = grad_pad[:, 1 - row_off:1 - row_off + grid_rows, :]
            moved = jnp.dot(weights[tap_index].T, earlier.reshape(feature_sequence, -1), preferred_element_type=jnp.float32)
            shifted_scale = tap_scale(rows_index - row_off, grid_rows)[tap_index]
            moved = moved.reshape(internal_embedding, grid_rows, longitudes) * shifted_scale[None, :, None]
            grad_total = grad_total + jnp.roll(moved, col_off, axis=2)
        return (weight_total + jnp.stack(updates), grad_total.astype(jnp.bfloat16))
    aggregate_coefficient, latent_derivative = lax.scan(adjoint_sweep, jnp.zeros((9, feature_sequence, internal_embedding), jnp.float32), (member_embedding, prediction_derivative))
    return (crps_objective, latent_derivative, aggregate_coefficient / tally_number)
```

```python
import functools
import math

import jax
import jax.numpy as jnp
from jax import lax
from jax.experimental import pallas as pl
from jax.experimental.pallas import tpu as pltpu
from jax.sharding import PartitionSpec as P

MESH = pl.DeviceIdType.MESH
F32 = jnp.float32
BF16 = jnp.bfloat16

CH, LATENT, LON, MEMBERS, NLAT = 100, 512, 720, 16, 32
LANES = 128
BLOCK = LON // MEMBERS
SLOT = 48
RING = 8
TAP_ROWS = 112
HALF = LATENT // 2
SMOOTHING = 0.01
PAIR_COEF = (1.0 - 0.05 / MEMBERS) / (MEMBERS - 1)
COLUMNS = (4, 0, 1, 2, 6, 7, 8, 3, 5)


def remote(src, dst, send_sem, recv_sem, device):
    return pltpu.make_async_remote_copy(
        src_ref=src, dst_ref=dst, send_sem=send_sem, recv_sem=recv_sem,
        device_id=device, device_id_type=MESH,
    )


def resplit(block):
    total = block[0:1] + block[1:2]
    lead = total.astype(BF16).astype(F32)
    row = lax.broadcasted_iota(jnp.int32, block.shape, 0)
    return jnp.where(row == 0, lead, jnp.where(row == 1, total - lead, block))


def kernel(area_ref, emb, w_ref, obs, d_ref, red,
           wp, ps, pr, fbuf, send_a, recv_a, vals, send_b, recv_b, gs, gr, gf, gcat,
           dwh, send_c, recv_c, s1, r1, s2, r2, s3, r3,
           h_send, h_recv, a_send, a_recv, b_send, b_recv, g_send, g_recv,
           c_send, c_recv, s1_send, s1_recv, s2_send, s2_recv, s3_send, s3_recv,
           t2_send, t2_recv, t1_send, t1_recv, tc_send, tc_recv):
    me = lax.axis_index("ens")
    row = lax.axis_index("space")
    x_lo, y = me // RING, me % RING
    core = row % 2
    z = (row // 2) % RING
    x_hi = row // (2 * RING)
    x = 2 * x_hi + x_lo
    up = (row + 1) % NLAT
    down = (row + NLAT - 1) % NLAT
    twin = (me, row + 1 - 2 * core)

    def at(x_, y_, z_):
        return ((x_ % 2) * RING + y_, ((x_ // 2) * RING + z_) * 2 + core)

    pos1 = y + core * (z - y)
    pos2 = z + core * (y - z)

    def ring1(p):
        return at(x, y + (1 - core) * (p - y), z + core * (p - z))

    def ring2(p):
        return at(x, y + core * (p - y), z + (1 - core) * (p - z))

    barrier = pltpu.get_barrier_semaphore()

    def greet(device):
        pl.semaphore_signal(barrier, inc=1, device_id=device, device_id_type=MESH)

    @pl.loop(1, MEMBERS)
    def _(i):
        greet(((me + i) % MEMBERS, row))

    @pl.loop(1, RING)
    def _(i):
        greet(at(x, y, (z + i) % RING))

    greet(at((x + 2) % 4, y, z))
    greet(at((x + 2) % 4 + 1 - 2 * (x % 2), y, z))
    greet(twin)
    greet((me, (row + 2 * core - 1 + NLAT) % NLAT))

    wp[...] = jnp.zeros_like(wp)
    for t in range(9):
        wp[t, 0:CH, :] = w_ref[t]

    latitude = math.pi * ((row.astype(F32) + 0.5) / NLAT - 0.5)
    east_west = 1.0 / (0.25 + jnp.cos(jnp.full((1, LANES), latitude, F32)))

    def product(first):
        mat = wp[first:first + 3].reshape(3 * LANES, LATENT)
        out = lax.dot_general(emb[...], mat, (((1,), (1,)), ((), ())), preferred_element_type=F32)
        return (pltpu.roll(out[:, 0:LANES], 1, 0), out[:, LANES:2 * LANES],
                pltpu.roll(out[:, 2 * LANES:3 * LANES], LON - 1, 0))

    west, mid, east = product(6)
    ps[0] = (west + mid + east).astype(BF16)
    pl.semaphore_wait(barrier, MEMBERS - 1 + RING - 1 + 4)
    to_down = remote(ps.at[0], pr.at[0], h_send.at[0], h_recv.at[0], (me, down))
    to_down.start()
    west, mid, east = product(0)
    ps[1] = (west + mid + east).astype(BF16)
    to_up = remote(ps.at[1], pr.at[1], h_send.at[1], h_recv.at[1], (me, up))
    to_up.start()
    west, mid, east = product(3)
    own = mid + east_west * (west + east)
    to_down.wait_recv()
    own = own + jnp.where(row < NLAT - 1, pr[0].astype(F32), 0.0)
    to_up.wait_recv()
    fbuf[0:LON, :] = own + jnp.where(row > 0, pr[1].astype(F32), 0.0)
    fbuf[LON:LON + 16, :] = jnp.zeros((16, LANES), F32)

    for k in range(MEMBERS):
        send_a[k] = fbuf[BLOCK * k:BLOCK * k + SLOT, :].astype(BF16)

    def a_copy(k, slot):
        return remote(send_a.at[k], recv_a.at[slot], a_send.at[k], a_recv.at[slot], (k, row))

    @pl.loop(1, MEMBERS)
    def _(i):
        a_copy((me + i) % MEMBERS, me).start()

    vals[me] = send_a[me].astype(F32)

    @pl.loop(1, MEMBERS)
    def _(i):
        k = (me + i) % MEMBERS
        a_copy(k, k).wait_recv()
        vals[k] = recv_a[k].astype(F32)

    area = area_ref[0]

    def score(j, loss):
        rows = pl.ds(pl.multiple_of(8 * j, 8), 8)
        f = [vals[i, rows, :] for i in range(MEMBERS)]
        o = obs[rows, :]
        grad, pair, total = [], [None] * MEMBERS, None
        pairs = None
        for i in range(MEMBERS):
            d = f[i] - o
            q = d * d + SMOOTHING
            r = lax.rsqrt(q)
            grad.append(d * r)
            total = q * r if total is None else total + q * r
        for i in range(MEMBERS):
            for k in range(i + 1, MEMBERS):
                d = f[i] - f[k]
                q = d * d + SMOOTHING
                r = lax.rsqrt(q)
                u = d * r
                pair[i] = u if pair[i] is None else pair[i] + u
                pair[k] = -u if pair[k] is None else pair[k] - u
                pairs = q * r if pairs is None else pairs + q * r
        for i in range(MEMBERS):
            vals[i, rows, :] = area * (grad[i] - PAIR_COEF * pair[i])
        crps = total - 0.5 * PAIR_COEF * (2.0 * pairs + MEMBERS * math.sqrt(SMOOTHING))
        lon = 8 * j + lax.broadcasted_iota(jnp.int32, (8, LANES), 0)
        ch = lax.broadcasted_iota(jnp.int32, (8, LANES), 1)
        return loss + jnp.where((lon < BLOCK) & (ch < CH), crps, 0.0)

    loss = lax.fori_loop(0, SLOT // 8, score, jnp.zeros((8, LANES), F32))
    loss = area * jnp.sum(loss)

    def b_copy(k, slot):
        return remote(send_b.at[k], recv_b.at[slot], b_send.at[k], b_recv.at[slot], (k, row))

    @pl.loop(1, MEMBERS)
    def _(i):
        k = (me + i) % MEMBERS
        send_b[k] = vals[k].astype(BF16)
        b_copy(k, me).start()

    recv_b[me] = vals[me].astype(BF16)

    sub = lax.broadcasted_iota(jnp.int32, (16, HALF), 0)
    lead = jnp.full((16, HALF), loss, F32).astype(BF16).astype(F32)
    tail = jnp.where(sub == 0, lead, jnp.where(sub == 1, loss - lead, 0.0))
    for h in range(2):
        dwh[h, 9 * TAP_ROWS:, :] = tail
        send_c[h, 9 * TAP_ROWS:, :] = tail.astype(BF16)

    @pl.loop(1, MEMBERS)
    def _(i):
        k = (me + i) % MEMBERS
        b_copy(k, k).wait_recv()

    def wrap(slot):
        gf[slot, 7:8, :] = gf[slot, LON + 7:LON + 8, :]
        gf[slot, LON + 8:LON + 9, :] = gf[slot, 8:9, :]

    for k in range(MEMBERS):
        gf[0, 8 + BLOCK * k:8 + BLOCK * k + SLOT, :] = recv_b[k].astype(F32)
    gs[...] = gf[0, 8:8 + LON, :].astype(BF16)
    g_down = remote(gs, gr.at[0], g_send.at[0], g_recv.at[0], (me, down))
    g_up = remote(gs, gr.at[1], g_send.at[1], g_recv.at[1], (me, up))
    g_down.start()
    g_up.start()
    wrap(0)

    def gather(slot, first):
        for b in range(3):
            column = COLUMNS.index(first + b) * LANES
            gcat[:, column:column + LANES] = gf[slot, 9 - b:9 - b + LON, :].astype(BF16)

    def outer(t):
        column = COLUMNS.index(t) * LANES
        out = lax.dot_general(gcat[:, column:column + LANES], emb[...], (((0,), (0,)), ((), ())),
                              preferred_element_type=F32)[0:TAP_ROWS]
        if t in (3, 5):
            out = out * east_west[:, 0:1]
        for h in range(2):
            part = out[:, HALF * h:HALF * (h + 1)]
            dwh[h, TAP_ROWS * t:TAP_ROWS * (t + 1), :] = part
            send_c[h, TAP_ROWS * t:TAP_ROWS * (t + 1), :] = part.astype(BF16)

    gather(0, 3)
    for t in (3, 4, 5):
        outer(t)
    g_down.wait_recv()
    gf[1, 8:8 + LON, :] = jnp.where(row < NLAT - 1, gr[0].astype(F32), 0.0)
    wrap(1)
    gather(1, 0)
    for t in (0, 1, 2):
        outer(t)
    g_up.wait_recv()
    gf[2, 8:8 + LON, :] = jnp.where(row > 0, gr[1].astype(F32), 0.0)
    wrap(2)
    gather(2, 6)
    for t in (6, 7, 8):
        outer(t)

    rows1 = RING * 16

    def c_copy(p):
        rows = pl.ds(pl.multiple_of(p * rows1, rows1), rows1)
        return remote(send_c.at[1 - core, rows], recv_c.at[rows], c_send.at[p], c_recv.at[p], twin)

    @pl.loop(0, RING)
    def _(i):
        c_copy((pos1 + 1 + i) % RING).start()

    def s1_copy(p, slot):
        return remote(s1.at[p], r1.at[slot], s1_send.at[p], s1_recv.at[slot], ring1(p))

    def chip_sum(p):
        c_copy(p).wait_recv()
        rows = pl.ds(pl.multiple_of(p * rows1, rows1), rows1)
        total = dwh[core, rows, :] + recv_c[rows, :].astype(F32)
        last = total[rows1 - 16:]
        last = jnp.where(p == RING - 1, resplit(last), last)
        return jnp.concatenate([total[:rows1 - 16], last], axis=0).astype(BF16)

    @pl.loop(1, RING)
    def _(i):
        p = (pos1 + i) % RING
        s1[p] = chip_sum(p)
        s1_copy(p, pos1).start()

    r1[pos1] = chip_sum(pos1)

    plain = jnp.concatenate([wp[t] for t in COLUMNS[:7]], axis=0)
    scaled = jnp.concatenate([wp[t] for t in COLUMNS[7:]], axis=0)
    moved = jnp.dot(gcat[:, 0:7 * LANES], plain, preferred_element_type=F32)
    moved_ew = jnp.dot(gcat[:, 7 * LANES:], scaled, preferred_element_type=F32)
    d_ref[...] = (moved + east_west[:, 0:1] * moved_ew).astype(BF16)

    @pl.loop(1, RING)
    def _(i):
        p = (pos1 + i) % RING
        s1_copy(p, p).wait_recv()

    total = r1[0].astype(F32)
    for p in range(1, RING):
        total = total + r1[p].astype(F32)
    last = total[rows1 - 16:]
    last = jnp.where(pos1 == RING - 1, resplit(last), last)
    for q in range(RING - 1):
        s2[q] = total[16 * q:16 * (q + 1)].astype(BF16)
    s2[RING - 1] = last.astype(BF16)

    def s2_copy(p, slot):
        return remote(s2.at[p], r2.at[slot], s2_send.at[p], s2_recv.at[slot], ring2(p))

    @pl.loop(1, RING)
    def _(i):
        s2_copy((pos2 + i) % RING, pos2).start()

    r2[pos2] = s2[pos2]

    @pl.loop(1, RING)
    def _(i):
        p = (pos2 + i) % RING
        s2_copy(p, p).wait_recv()

    special = (pos1 == RING - 1) & (pos2 == RING - 1)
    total = r2[0].astype(F32)
    for p in range(1, RING):
        total = total + r2[p].astype(F32)
    total = jnp.where(special, resplit(total), total).astype(BF16)
    s3[...] = total

    def s3_copy(i, slot):
        p = (x + i) % 4
        return remote(s3, r3.at[slot], s3_send.at[i], s3_recv.at[slot], at(p, y, z))

    @pl.loop(1, 4)
    def _(i):
        s3_copy(i, x).start()

    r3[x] = total

    @pl.loop(1, 4)
    def _(i):
        s3_copy(i, (x + i) % 4).wait_recv()

    total = (r3[0].astype(F32) + r3[1].astype(F32)) + (r3[2].astype(F32) + r3[3].astype(F32))
    total = jnp.where(special, resplit(total), total).astype(BF16)
    red[core, pos1, pos2] = total

    def t2_copy(i, slot):
        block = red.at[core, pos1, slot]
        return remote(block, block, t2_send.at[i], t2_recv.at[slot], ring2((pos2 + i) % RING))

    @pl.loop(1, RING)
    def _(i):
        t2_copy(i, pos2).start()

    @pl.loop(1, RING)
    def _(i):
        t2_copy(i, (pos2 + i) % RING).wait_recv()

    def t1_copy(i, slot):
        block = red.at[core, slot]
        return remote(block, block, t1_send.at[i], t1_recv.at[slot], ring1((pos1 + i) % RING))

    @pl.loop(1, RING)
    def _(i):
        t1_copy(i, pos1).start()

    def tc_copy(half, p):
        block = red.at[half, p]
        return remote(block, block, tc_send.at[p], tc_recv.at[p], twin)

    tc_copy(core, pos1).start()

    @pl.loop(1, RING)
    def _(i):
        p = (pos1 + i) % RING
        t1_copy(i, p).wait_recv()
        tc_copy(core, p).start()

    @pl.loop(0, RING)
    def _(p):
        tc_copy(1 - core, p).wait_recv()

    to_down.wait_send()
    to_up.wait_send()
    g_down.wait_send()
    g_up.wait_send()

    @pl.loop(1, MEMBERS)
    def _(i):
        k = (me + i) % MEMBERS
        a_copy(k, me).wait_send()
        b_copy(k, me).wait_send()

    @pl.loop(0, RING)
    def _(p):
        c_copy(p).wait_send()
        tc_copy(core, p).wait_send()

    @pl.loop(1, RING)
    def _(i):
        s1_copy((pos1 + i) % RING, pos1).wait_send()
        s2_copy((pos2 + i) % RING, pos2).wait_send()
        t2_copy(i, pos2).wait_send()
        t1_copy(i, pos1).wait_send()

    @pl.loop(1, 4)
    def _(i):
        s3_copy(i, x).wait_send()


def per_device(member_embedding, weights, verifying_observed_grid, area_weight):
    emb = member_embedding[0, :, 0, :].T
    obs = jnp.pad(verifying_observed_grid[:, 0, :].T, ((0, SLOT - BLOCK), (0, LANES - CH)))
    vmem = pl.BlockSpec(memory_space=pltpu.VMEM)
    dma = lambda n: pltpu.SemaphoreType.DMA((n,))
    scratch = [
        pltpu.VMEM((9, LANES, LATENT), BF16),
        pltpu.VMEM((2, LON, LANES), BF16),
        pltpu.VMEM((2, LON, LANES), BF16),
        pltpu.VMEM((LON + 16, LANES), F32),
        pltpu.VMEM((MEMBERS, SLOT, LANES), BF16),
        pltpu.VMEM((MEMBERS, SLOT, LANES), BF16),
        pltpu.VMEM((MEMBERS, SLOT, LANES), F32),
        pltpu.VMEM((MEMBERS, SLOT, LANES), BF16),
        pltpu.VMEM((MEMBERS, SLOT, LANES), BF16),
        pltpu.VMEM((LON, LANES), BF16),
        pltpu.VMEM((2, LON, LANES), BF16),
        pltpu.VMEM((3, LON + 32, LANES), F32),
        pltpu.VMEM((LON, 9 * LANES), BF16),
        pltpu.VMEM((2, RING * RING * 16, HALF), F32),
        pltpu.VMEM((2, RING * RING * 16, HALF), BF16),
        pltpu.VMEM((RING * RING * 16, HALF), BF16),
        pltpu.VMEM((RING, RING * 16, HALF), BF16),
        pltpu.VMEM((RING, RING * 16, HALF), BF16),
        pltpu.VMEM((RING, 16, HALF), BF16),
        pltpu.VMEM((RING, 16, HALF), BF16),
        pltpu.VMEM((16, HALF), BF16),
        pltpu.VMEM((4, 16, HALF), BF16),
    ]
    sems = [dma(n) for n in (2, 2, 16, 16, 16, 16, 2, 2, 8, 8, 8, 8, 8, 8, 4, 4, 8, 8, 8, 8, 8, 8)]
    moved, red = pl.pallas_call(
        kernel,
        out_shape=(jax.ShapeDtypeStruct((LON, LATENT), BF16),
                   jax.ShapeDtypeStruct((2, RING, RING, 16, HALF), BF16)),
        in_specs=[pl.BlockSpec(memory_space=pltpu.SMEM), vmem, vmem, vmem],
        out_specs=(vmem, vmem),
        scratch_shapes=scratch + sems,
        compiler_params=pltpu.CompilerParams(
            collective_id=0, has_side_effects=True, vmem_limit_bytes=48 * 1024 * 1024),
        cost_estimate=pl.CostEstimate(flops=2_600_000_000, bytes_accessed=6_000_000, transcendentals=1_000_000),
        name="decoder",
    )(area_weight, emb, weights, obs)
    red = red.reshape(2, RING * RING * 16, HALF)
    tally = MEMBERS * NLAT * LON
    tail = red[0, 9 * TAP_ROWS:9 * TAP_ROWS + 2, 0].astype(F32)
    objective = (tail[0] + tail[1]) / tally
    both = red[:, :9 * TAP_ROWS].reshape(2, 9, TAP_ROWS, HALF)[:, :, :CH].astype(F32) / tally
    grad_weight = jnp.concatenate([both[0], both[1]], axis=-1)
    return objective, moved.T[None, :, None, :], grad_weight


def solution(mesh):
    return jax.shard_map(
        per_device,
        mesh=mesh,
        in_specs=(P("ens", None, "space", None), P(), P(None, "space", "ens"), P("space")),
        out_specs=(P(), P("ens", None, "space", None), P()),
        check_vma=False,
    )
```

```python
import math

import jax
import jax.numpy as jnp
from jax import lax
from jax.experimental import pallas as pl
from jax.experimental.pallas import tpu as pltpu
from jax.sharding import PartitionSpec as P

MESH = pl.DeviceIdType.MESH
F32 = jnp.float32
BF16 = jnp.bfloat16

CH, LATENT, LON, MEMBERS, NLAT = 100, 512, 720, 16, 32
LANES = 128
BLOCK = LON // MEMBERS
SLOT = 48
RING = 8
HALF = LATENT // 2
SUM_ROWS = 512
SMOOTHING = 0.01
PAIR_COEF = (1.0 - 0.05 / MEMBERS) / (MEMBERS - 1)
TALLY = MEMBERS * NLAT * LON
COLUMNS = (4, 0, 1, 2, 6, 7, 8, 3, 5)
GROUPS = ((3, 4, 5, 0), (1, 2, 6, 7, 8))
SHAPES = ((4, 8), (8, 4))


def remote(src, dst, send_sem, recv_sem, device):
    return pltpu.make_async_remote_copy(
        src_ref=src, dst_ref=dst, send_sem=send_sem, recv_sem=recv_sem,
        device_id=device, device_id_type=MESH,
    )


def far(i, size):
    odd = i % 2
    return size // 2 + (i // 2) * (1 - odd) - ((i + 1) // 2) * odd


def resplit(block):
    total = block[0:1] + block[1:2]
    lead = total.astype(BF16).astype(F32)
    row = lax.broadcasted_iota(jnp.int32, block.shape, 0)
    return jnp.where(row == 0, lead, jnp.where(row == 1, total - lead, block))


class Flow:
    def __init__(self, shape, core, twin, pos, rings, has_loss, dw, bufs, red, sems):
        self.first, self.second = shape
        self.core, self.twin = core, twin
        self.pos, self.rings = pos, rings
        self.has_loss = has_loss
        self.dw, self.red = dw, red
        self.send_c, self.recv_c, self.s1, self.r1, self.s2, self.r2, self.s3, self.r3 = bufs
        self.sems = sems
        self.rows = 16 * self.second

    def copy(self, phase, src, dst, send, recv, device):
        return remote(src, dst, self.sems[2 * phase].at[send], self.sems[2 * phase + 1].at[recv], device)

    def c_copy(self, p):
        return self.copy(0, self.send_c.at[p], self.recv_c.at[p], p, p, self.twin)

    def s1_copy(self, p, slot):
        return self.copy(1, self.s1.at[p], self.r1.at[slot], p, slot, self.rings[0](p))

    def s2_copy(self, p, slot):
        return self.copy(2, self.s2.at[p], self.r2.at[slot], p, slot, self.rings[1](p))

    def s3_copy(self, p, slot):
        return self.copy(3, self.s3, self.r3.at[slot], p, slot, self.rings[2](p))

    def t2_copy(self, p, slot):
        block = self.red.at[self.core, self.pos[0], slot]
        return self.copy(4, block, block, p, slot, self.rings[1](p))

    def t1_copy(self, p, slot):
        block = self.red.at[self.core, slot]
        return self.copy(5, block, block, p, slot, self.rings[0](p))

    def tc_copy(self, half, p):
        block = self.red.at[half, p]
        return self.copy(6, block, block, p, p, self.twin)

    def peers(self, ring, body, near=False):
        size = (self.first, self.second, RING)[ring]

        @pl.loop(0, size - 1)
        def _(i):
            body((self.pos[ring] + far(size - 2 - i if near else i, size)) % size)

    def start(self):
        other = self.dw.at[1 - self.core]
        for p in range(self.first):
            self.send_c[p] = other[p * self.rows:(p + 1) * self.rows, :].astype(BF16)
        self.peers(0, lambda p: self.c_copy(p).start())
        self.c_copy(self.pos[0]).start()

    def chip_sum(self, p):
        self.c_copy(p).wait_recv()
        rows = pl.ds(pl.multiple_of(p * self.rows, self.rows), self.rows)
        total = self.dw[self.core, rows, :] + self.recv_c[p].astype(F32)
        if self.has_loss:
            last = total[self.rows - 16:]
            last = jnp.where(p == self.first - 1, resplit(last), last)
            total = jnp.concatenate([total[:self.rows - 16], last], axis=0)
        return total.astype(BF16)

    def step1(self):
        def send(p):
            self.s1[p] = self.chip_sum(p)
            self.s1_copy(p, self.pos[0]).start()

        self.peers(0, send)
        self.r1[self.pos[0]] = self.chip_sum(self.pos[0])

    def step2(self):
        self.peers(0, lambda p: self.s1_copy(p, p).wait_recv(), near=True)
        total = self.r1[0].astype(F32)
        for p in range(1, self.first):
            total = total + self.r1[p].astype(F32)
        for q in range(self.second):
            block = total[16 * q:16 * (q + 1)]
            if self.has_loss and q == self.second - 1:
                block = jnp.where(self.pos[0] == self.first - 1, resplit(block), block)
            self.s2[q] = block.astype(BF16)
        self.peers(1, lambda p: self.s2_copy(p, self.pos[1]).start())
        self.r2[self.pos[1]] = self.s2[self.pos[1]]

    def special(self, block):
        if not self.has_loss:
            return block
        here = (self.pos[0] == self.first - 1) & (self.pos[1] == self.second - 1)
        return jnp.where(here, resplit(block), block)

    def step3(self):
        self.peers(1, lambda p: self.s2_copy(p, p).wait_recv(), near=True)
        total = self.r2[0].astype(F32)
        for p in range(1, self.second):
            total = total + self.r2[p].astype(F32)
        total = self.special(total).astype(BF16)
        self.s3[...] = total
        self.peers(2, lambda p: self.s3_copy(p, self.pos[2]).start())
        self.r3[self.pos[2]] = total

    def step4(self):
        self.peers(2, lambda p: self.s3_copy(p, p).wait_recv(), near=True)
        total = self.r3[0].astype(F32)
        for p in range(1, RING):
            total = total + self.r3[p].astype(F32)
        self.red[self.core, self.pos[0], self.pos[1]] = self.special(total).astype(BF16)
        self.peers(1, lambda p: self.t2_copy(p, self.pos[1]).start())

    def step5(self):
        self.peers(1, lambda p: self.t2_copy(p, p).wait_recv(), near=True)
        self.peers(0, lambda p: self.t1_copy(p, self.pos[0]).start())
        self.tc_copy(self.core, self.pos[0]).start()

    def step6(self):
        def forward(p):
            self.t1_copy(p, p).wait_recv()
            self.tc_copy(self.core, p).start()

        self.peers(0, forward, near=True)

    def finish(self):
        @pl.loop(0, self.first)
        def _(p):
            self.tc_copy(1 - self.core, p).wait_recv()

        @pl.loop(0, self.first)
        def _(p):
            self.c_copy(p).wait_send()
            self.tc_copy(self.core, p).wait_send()

        def first(p):
            self.s1_copy(p, self.pos[0]).wait_send()
            self.t1_copy(p, self.pos[0]).wait_send()

        def second(p):
            self.s2_copy(p, self.pos[1]).wait_send()
            self.t2_copy(p, self.pos[1]).wait_send()

        self.peers(0, first)
        self.peers(1, second)
        self.peers(2, lambda p: self.s3_copy(p, self.pos[2]).wait_send())


def kernel(area_ref, emb_hbm, w_hbm, obs_hbm, d_ref, red0, red1, *scratch):
    (emb, w_ref, obs_raw, obs, wp, fbuf, pown, ps, pr, send_a, recv_a, vals, send_b, recv_b, hr, gf, gcat,
     dw0, dw1) = scratch[:19]
    bufs = (scratch[19:27], scratch[27:35])
    load, h_send, h_recv, a_send, a_recv, b_send, b_recv, g_send, g_recv = scratch[35:44]
    sums = (scratch[44:58], scratch[58:72])

    me = lax.axis_index("ens")
    row = lax.axis_index("space")
    x_lo, y = me // RING, me % RING
    core = row % 2
    z = (row // 2) % RING
    x_hi = row // (2 * RING)
    x = 2 * x_hi + x_lo
    twin = (me, row + 1 - 2 * core)
    next_row = (row + 2 * core - 1 + NLAT) % NLAT
    other = (me, next_row)
    inner = (row > 0) & (row < NLAT - 1)

    loads = [pltpu.make_async_copy(src, dst, load.at[i])
             for i, (src, dst) in enumerate(((w_hbm, w_ref), (emb_hbm, emb), (obs_hbm, obs_raw)))]
    for copy in loads:
        copy.start()

    def at(x_, y_, z_):
        return ((x_ % 2) * RING + y_, ((x_ // 2) * RING + z_) * 2 + core)

    barrier = pltpu.get_barrier_semaphore()

    def greet(device):
        pl.semaphore_signal(barrier, inc=1, device_id=device, device_id_type=MESH)

    def member(j):
        return ((x_lo + 1 - j % 2) % 2) * RING + (y + far(j // 2, RING)) % RING

    greet(other)
    greet(twin)

    @pl.loop(0, MEMBERS - 1)
    def _(j):
        greet((member(j), row))

    @pl.loop(0, RING - 1)
    def _(i):
        greet(at(x, y, (z + far(i, RING)) % RING))

    greet(at((x + 2) % 4, y, z))
    greet(at((x + 2) % 4 + 1 - 2 * (x % 2), y, z))

    for t in range(9):
        wp[t, 96:, :] = jnp.zeros((LANES - 96, LATENT), BF16)
    fbuf[LON:LON + 16, :] = jnp.zeros((16, LANES), F32)
    obs[...] = jnp.zeros_like(obs)
    loads[0].wait()
    for t in range(9):
        wp[t, 0:CH, :] = w_ref[t]
    loads[1].wait()

    latitude = math.pi * ((row.astype(F32) + 0.5) / NLAT - 0.5)
    east_west = 1.0 / (0.25 + jnp.cos(jnp.full((1, LANES), latitude, F32)))

    def product(first):
        mat = wp[pl.ds(first, 3)].reshape(3 * LANES, LATENT)
        out = lax.dot_general(emb[...], mat, (((1,), (1,)), ((), ())), preferred_element_type=F32)
        return (pltpu.roll(out[:, 0:LANES], 1, 0), out[:, LANES:2 * LANES],
                pltpu.roll(out[:, 2 * LANES:3 * LANES], LON - 1, 0))

    def h_copy(slot, k):
        return remote(ps.at[slot, k], pr.at[slot, k], h_send.at[slot, k], h_recv.at[slot, k], (other, twin)[slot])

    for slot in range(2):
        lower = (1 - core) if slot == 0 else core
        west, mid, east = product(6 * lower)
        fbuf[0:LON, :] = west + mid + east
        for k in range(MEMBERS):
            ps[slot, k] = fbuf[BLOCK * k:BLOCK * k + SLOT, :].astype(BF16)
        if slot == 0:
            pl.semaphore_wait(barrier, MEMBERS - 1 + RING - 1 + 4)

        @pl.loop(0, MEMBERS)
        def _(j):
            h_copy(slot, member(j)).start()

    west, mid, east = product(3)
    fbuf[0:LON, :] = mid + east_west * (west + east)
    for k in range(MEMBERS):
        pown[k] = fbuf[BLOCK * k:BLOCK * k + SLOT, :]

    def a_copy(k, slot):
        return remote(send_a.at[k], recv_a.at[slot], a_send.at[k], a_recv.at[slot], (k, row))

    def forecast(k):
        h_copy(1, k).wait_recv()
        h_copy(0, k).wait_recv()
        total = pown[k] + pr[1, k].astype(F32)
        return (total + jnp.where(inner, pr[0, k].astype(F32), 0.0)).astype(BF16)

    @pl.loop(0, MEMBERS - 1)
    def _(j):
        k = member(j)
        send_a[k] = forecast(k)
        a_copy(k, me).start()

    vals[me] = forecast(me).astype(F32)

    loads[2].wait()
    for i in range(BLOCK):
        obs[i:i + 1, 0:CH] = obs_raw[i]

    @pl.loop(0, MEMBERS - 1)
    def _(j):
        k = member(MEMBERS - 2 - j)
        a_copy(k, k).wait_recv()
        vals[k] = recv_a[k].astype(F32)

    area = area_ref[0]

    def score(j, loss):
        rows = pl.ds(pl.multiple_of(8 * j, 8), 8)
        f = [vals[i, rows, :] for i in range(MEMBERS)]
        o = obs[rows, :]
        grad, pair, total = [], [None] * MEMBERS, None
        pairs = None
        for i in range(MEMBERS):
            d = f[i] - o
            q = d * d + SMOOTHING
            r = lax.rsqrt(q)
            grad.append(d * r)
            total = q * r if total is None else total + q * r
        for i in range(MEMBERS):
            for k in range(i + 1, MEMBERS):
                d = f[i] - f[k]
                q = d * d + SMOOTHING
                r = lax.rsqrt(q)
                u = d * r
                pair[i] = u if pair[i] is None else pair[i] + u
                pair[k] = -u if pair[k] is None else pair[k] - u
                pairs = q * r if pairs is None else pairs + q * r
        for i in range(MEMBERS):
            vals[i, rows, :] = area * (grad[i] - PAIR_COEF * pair[i])
        crps = total - 0.5 * PAIR_COEF * (2.0 * pairs + MEMBERS * math.sqrt(SMOOTHING))
        lon = 8 * j + lax.broadcasted_iota(jnp.int32, (8, LANES), 0)
        ch = lax.broadcasted_iota(jnp.int32, (8, LANES), 1)
        return loss + jnp.where((lon < BLOCK) & (ch < CH), crps, 0.0)

    loss = lax.fori_loop(0, SLOT // 8, score, jnp.zeros((8, LANES), F32))

    def b_copy(k, slot):
        return remote(send_b.at[k], recv_b.at[slot], b_send.at[k], b_recv.at[slot], (k, row))

    @pl.loop(0, MEMBERS - 1)
    def _(j):
        k = member(j)
        send_b[k] = vals[k].astype(BF16)
        b_copy(k, me).start()

    recv_b[me] = vals[me].astype(BF16)

    loss = area * jnp.sum(loss)
    sub = lax.broadcasted_iota(jnp.int32, (16, HALF), 0)
    lead = jnp.full((16, HALF), loss, F32).astype(BF16).astype(F32)
    tail = jnp.where(sub == 0, lead, jnp.where(sub == 1, loss - lead, 0.0))
    for h in range(2):
        dw0[h, CH * len(GROUPS[0]):SUM_ROWS - 16, :] = jnp.zeros((SUM_ROWS - 16 - CH * len(GROUPS[0]), HALF), F32)
        dw0[h, SUM_ROWS - 16:, :] = tail
        dw1[h, CH * len(GROUPS[1]):, :] = jnp.zeros((SUM_ROWS - CH * len(GROUPS[1]), HALF), F32)

    def g_copy(slot, k, device):
        return remote(recv_b.at[k], hr.at[slot, k], g_send.at[slot, k], g_recv.at[slot, k], device)

    g_copy(0, me, other).start()
    g_copy(1, me, twin).start()

    @pl.loop(0, MEMBERS - 1)
    def _(j):
        k = member(MEMBERS - 2 - j)
        b_copy(k, k).wait_recv()
        g_copy(0, k, other).start()
        g_copy(1, k, twin).start()

    def gather(slot, first, block):
        for k in range(MEMBERS):
            gf[slot, 8 + BLOCK * k:8 + BLOCK * k + SLOT, :] = block(k).astype(F32)
        gf[slot, 7:8, :] = gf[slot, LON + 7:LON + 8, :]
        gf[slot, LON + 8:LON + 9, :] = gf[slot, 8:9, :]
        for b in range(3):
            column = COLUMNS.index(first + b) * LANES
            gcat[:, column:column + LANES] = gf[slot, 9 - b:9 - b + LON, :].astype(BF16)

    def outer(t):
        column = COLUMNS.index(t) * LANES
        out = lax.dot_general(gcat[:, column:column + LANES], emb[...], (((0,), (0,)), ((), ())),
                              preferred_element_type=F32)[0:CH]
        if t in (3, 5):
            out = out * east_west[:, 0:1]
        group = 0 if t in GROUPS[0] else 1
        base = GROUPS[group].index(t) * CH
        for h in range(2):
            (dw0, dw1)[group][h, base:base + CH, :] = out[:, HALF * h:HALF * (h + 1)]

    def neighbour(slot, keep):
        @pl.loop(0, MEMBERS)
        def _(k):
            g_copy(slot, k, twin).wait_recv()

        return lambda k: jnp.where(keep, hr[slot, k].astype(F32), 0.0)

    def ring_a(p):
        return at(x, y + (1 - core) * (p - y), z + core * (p - z))

    def ring_b(p):
        return at(x, y + core * (p - y), z + (1 - core) * (p - z))

    def ring_x(p):
        return at(p, y, z)

    pos_a = y + core * (z - y)
    pos_b = z + core * (y - z)
    flows = (
        Flow(SHAPES[0], core, twin, (x, pos_a, pos_b), (ring_x, ring_a, ring_b), True, dw0, bufs[0], red0, sums[0]),
        Flow(SHAPES[1], core, twin, (pos_a, x, pos_b), (ring_a, ring_x, ring_b), False, dw1, bufs[1], red1, sums[1]),
    )

    gather(0, 3, lambda k: recv_b[k])
    for t in (3, 4, 5):
        outer(t)
    gather(1, 0, neighbour(1 - core, row < NLAT - 1))
    outer(0)
    flows[0].start()
    for t in (1, 2):
        outer(t)
    gather(2, 6, neighbour(core, row > 0))
    for t in (6, 7, 8):
        outer(t)
    flows[1].start()
    flows[0].step1()
    flows[1].step1()

    plain = jnp.concatenate([wp[t] for t in COLUMNS[:7]], axis=0)
    scaled = jnp.concatenate([wp[t] for t in COLUMNS[7:]], axis=0)
    moved = jnp.dot(gcat[:, 0:7 * LANES], plain, preferred_element_type=F32)
    moved_ew = jnp.dot(gcat[:, 7 * LANES:], scaled, preferred_element_type=F32)
    d_ref[...] = (moved + east_west[:, 0:1] * moved_ew).astype(BF16)

    for flow in flows:
        flow.step2()
    for flow in flows:
        flow.step3()
    for flow in flows:
        flow.step4()
    for flow in flows:
        flow.step5()
    for flow in flows:
        flow.step6()

    for flow in flows:
        flow.finish()

    @pl.loop(0, MEMBERS)
    def _(k):
        for slot in range(2):
            h_copy(slot, k).wait_send()
            g_copy(slot, k, twin).wait_send()

    @pl.loop(0, MEMBERS - 1)
    def _(j):
        k = member(j)
        a_copy(k, me).wait_send()
        b_copy(k, me).wait_send()


def unpack(d_ref, red0, red1, loss_ref, d_hbm, dw_hbm, buf, out, sem):
    move = pltpu.make_async_copy(d_ref, d_hbm, sem.at[9])
    move.start()
    for g, red in enumerate((red0, red1)):
        for h in range(2):
            buf[g, h] = red[h].reshape(SUM_ROWS, HALF).astype(F32)
    loss_ref[0] = jnp.sum(buf[0, 0, SUM_ROWS - 16:SUM_ROWS - 14, 0:1]) * (1.0 / TALLY)
    copies = []
    for g in range(2):
        for i, t in enumerate(GROUPS[g]):
            for h in range(2):
                out[t, :, HALF * h:HALF * (h + 1)] = buf[g, h, CH * i:CH * (i + 1), :] * (1.0 / TALLY)
            copies.append(pltpu.make_async_copy(out.at[t], dw_hbm.at[t], sem.at[t]))
            copies[-1].start()
    for copy in copies:
        copy.wait()
    move.wait()


def per_device(member_embedding, weights, verifying_observed_grid, area_weight):
    emb = member_embedding[0, :, 0, :].T
    obs = jnp.transpose(verifying_observed_grid, (2, 1, 0))
    vmem = pl.BlockSpec(memory_space=pltpu.VMEM)
    smem = pl.BlockSpec(memory_space=pltpu.SMEM)
    hbm = pl.BlockSpec(memory_space=pltpu.HBM)
    dma = lambda *n: pltpu.SemaphoreType.DMA(n)
    blocks = lambda kind: pltpu.VMEM((MEMBERS, SLOT, LANES), kind)
    scratch = [
        pltpu.VMEM((LON, LATENT), BF16),
        pltpu.VMEM((9, CH, LATENT), BF16),
        pltpu.VMEM((BLOCK, 1, CH), F32),
        pltpu.VMEM((SLOT, LANES), F32),
        pltpu.VMEM((9, LANES, LATENT), BF16),
        pltpu.VMEM((LON + 16, LANES), F32),
        blocks(F32),
        pltpu.VMEM((2, MEMBERS, SLOT, LANES), BF16),
        pltpu.VMEM((2, MEMBERS, SLOT, LANES), BF16),
        blocks(BF16),
        blocks(BF16),
        blocks(F32),
        blocks(BF16),
        blocks(BF16),
        pltpu.VMEM((2, MEMBERS, SLOT, LANES), BF16),
        pltpu.VMEM((3, LON + 32, LANES), F32),
        pltpu.VMEM((LON, 9 * LANES), BF16),
        pltpu.VMEM((2, SUM_ROWS, HALF), F32),
        pltpu.VMEM((2, SUM_ROWS, HALF), F32),
    ]
    for first, second in SHAPES:
        big = pltpu.VMEM((first, 16 * second, HALF), BF16)
        small = pltpu.VMEM((second, 16, HALF), BF16)
        scratch += [big, big, big, big, small, small, pltpu.VMEM((16, HALF), BF16), pltpu.VMEM((RING, 16, HALF), BF16)]
    scratch += [dma(3), dma(2, MEMBERS), dma(2, MEMBERS), dma(MEMBERS), dma(MEMBERS), dma(MEMBERS), dma(MEMBERS),
                dma(2, MEMBERS), dma(2, MEMBERS)]
    for first, second in SHAPES:
        for size in (first, first, second, RING, second, first, first):
            scratch += [dma(size), dma(size)]
    moved, red0, red1 = pl.pallas_call(
        kernel,
        out_shape=(jax.ShapeDtypeStruct((LON, LATENT), BF16),
                   *(jax.ShapeDtypeStruct((2, *shape, 16, HALF), BF16) for shape in SHAPES)),
        in_specs=[smem, hbm, hbm, hbm],
        out_specs=(vmem, vmem, vmem),
        scratch_shapes=scratch,
        compiler_params=pltpu.CompilerParams(
            collective_id=0, has_side_effects=True, vmem_limit_bytes=48 * 1024 * 1024),
        cost_estimate=pl.CostEstimate(flops=2_600_000_000, bytes_accessed=6_000_000, transcendentals=1_000_000),
        name="decoder",
    )(area_weight, *(pltpu.with_memory_space_constraint(a, pltpu.HBM) for a in (emb, weights, obs)))
    loss, moved, grad_weight = pl.pallas_call(
        unpack,
        out_shape=(jax.ShapeDtypeStruct((1,), F32), jax.ShapeDtypeStruct((LON, LATENT), BF16),
                   jax.ShapeDtypeStruct((9, CH, LATENT), F32)),
        in_specs=[vmem, vmem, vmem],
        out_specs=(smem, hbm, hbm),
        scratch_shapes=[pltpu.VMEM((2, 2, SUM_ROWS, HALF), F32), pltpu.VMEM((9, CH, LATENT), F32), dma(10)],
        compiler_params=pltpu.CompilerParams(vmem_limit_bytes=32 * 1024 * 1024),
        cost_estimate=pl.CostEstimate(flops=1_000_000, bytes_accessed=4_500_000, transcendentals=0),
        name="unpack",
    )(moved, red0, red1)
    return loss.reshape(()), moved.T[None, :, None, :], grad_weight


def solution(mesh):
    return jax.shard_map(
        per_device,
        mesh=mesh,
        in_specs=(P("ens", None, "space", None), P(), P(None, "space", "ens"), P("space")),
        out_specs=(P(), P("ens", None, "space", None), P()),
        check_vma=False,
    )
```

```python
import math

import jax
import jax.numpy as jnp
from jax import lax
from jax.experimental import pallas as pl
from jax.experimental.pallas import tpu as pltpu
from jax.sharding import PartitionSpec as P

MESH = pl.DeviceIdType.MESH
F32 = jnp.float32
BF16 = jnp.bfloat16

CH, LATENT, LON, MEMBERS, NLAT = 100, 512, 720, 16, 32
LANES = 128
BLOCK = LON // MEMBERS
SLOT = 48
RING = 8
HALF = LATENT // 2
SUM_ROWS = 512
PIECES = 5
PIECE = LON // PIECES
SMOOTHING = 0.01
PAIR_COEF = (1.0 - 0.05 / MEMBERS) / (MEMBERS - 1)
TALLY = MEMBERS * NLAT * LON
MIDDLE = (4, 3, 5)
UNITS = (((0, 0),), ((0, 1), (1, 0), (1, 1), (2, 0), (2, 1)))
MID_ROWS = 304
SHAPES = ((4, 8), (8, 4))


def steps(first, end):
    return pl.loop(first, end, unroll=True)


def remote(src, dst, send_sem, recv_sem, device):
    return pltpu.make_async_remote_copy(
        src_ref=src, dst_ref=dst, send_sem=send_sem, recv_sem=recv_sem,
        device_id=device, device_id_type=MESH,
    )


def far(i, size):
    odd = i % 2
    return size // 2 + (i // 2) * (1 - odd) - ((i + 1) // 2) * odd


def resplit(block):
    total = block[0:1] + block[1:2]
    lead = total.astype(BF16).astype(F32)
    row = lax.broadcasted_iota(jnp.int32, block.shape, 0)
    return jnp.where(row == 0, lead, jnp.where(row == 1, total - lead, block))


class Flow:
    def __init__(self, shape, pos, rings, has_loss, dw, bufs, sems):
        self.first, self.second = shape
        self.pos, self.rings = pos, rings
        self.has_loss = has_loss
        self.dw = dw
        self.s1, self.r1, self.s2, self.r2 = bufs
        self.sems = sems
        self.rows = 16 * self.second

    def copy(self, phase, src, dst, send, recv, device):
        return remote(src, dst, self.sems[2 * phase].at[send], self.sems[2 * phase + 1].at[recv], device)

    def s1_copy(self, p, slot):
        return self.copy(0, self.s1.at[p], self.r1.at[slot], p, slot, self.rings[0](p))

    def s2_copy(self, p, slot):
        return self.copy(1, self.s2.at[p], self.r2.at[slot], p, slot, self.rings[1](p))

    def peers(self, ring, body, near=False):
        size = (self.first, self.second)[ring]

        @steps(0, size - 1)
        def _(i):
            body((self.pos[ring] + far(size - 2 - i if near else i, size)) % size)

    def step1(self):
        for p in range(self.first):
            self.s1[p] = self.dw[p * self.rows:(p + 1) * self.rows, :].astype(BF16)
        self.peers(0, lambda p: self.s1_copy(p, self.pos[0]).start())
        self.r1[self.pos[0]] = self.s1[self.pos[0]]

    def step2(self):
        self.peers(0, lambda p: self.s1_copy(p, p).wait_recv(), near=True)
        total = self.r1[0].astype(F32)
        for p in range(1, self.first):
            total = total + self.r1[p].astype(F32)
        for q in range(self.second):
            block = total[16 * q:16 * (q + 1)]
            if self.has_loss and q == self.second - 1:
                block = jnp.where(self.pos[0] == self.first - 1, resplit(block), block)
            self.s2[q] = block.astype(BF16)
        self.peers(1, lambda p: self.s2_copy(p, self.pos[1]).start())
        self.r2[self.pos[1]] = self.s2[self.pos[1]]

    def special(self, block):
        if not self.has_loss:
            return block
        here = (self.pos[0] == self.first - 1) & (self.pos[1] == self.second - 1)
        return jnp.where(here, resplit(block), block)

    def step3(self):
        self.peers(1, lambda p: self.s2_copy(p, p).wait_recv(), near=True)
        total = self.r2[0].astype(F32)
        for p in range(1, self.second):
            total = total + self.r2[p].astype(F32)
        return self.special(total).astype(BF16)

    def finish(self):
        self.peers(0, lambda p: self.s1_copy(p, self.pos[0]).wait_send())
        self.peers(1, lambda p: self.s2_copy(p, self.pos[1]).wait_send())


def kernel(area_ref, emb_hbm, w_hbm, obs_hbm, d_ref, red, *scratch):
    (emb, halo, w_ref, obs_raw, obs, wp, fbuf, pown, ps, pr, send_a, recv_a, vals, send_b, recv_b, hr, gf, gcat,
     mid_sum, send_c, recv_c, dw0, dw1) = scratch[:23]
    s3, r3 = scratch[23:25]
    bufs = (scratch[25:29], scratch[29:33])
    (load, h_send, h_recv, e_send, e_recv, a_send, a_recv, b_send, b_recv, g_send, g_recv, c_sem,
     s3_send, s3_recv, ta_send, tx_send, t_recv, tc_send, tc_recv) = scratch[33:52]
    sums = (scratch[52:56], scratch[56:60])

    me = lax.axis_index("ens")
    row = lax.axis_index("space")
    x_lo, y = me // RING, me % RING
    core = row % 2
    z = (row // 2) % RING
    x_hi = row // (2 * RING)
    x = 2 * x_hi + x_lo
    twin = (me, row + 1 - 2 * core)
    next_row = (row + 2 * core - 1 + NLAT) % NLAT
    other = (me, next_row)
    inner = (row > 0) & (row < NLAT - 1)

    order = [3 * ((2 * (1 - core) + i * (1 + core)) % 3) for i in range(3)]
    w_loads = [pltpu.make_async_copy(w_hbm.at[pl.ds(t, 3)], w_ref.at[pl.ds(t, 3)], load.at[i])
               for i, t in enumerate(order)]
    emb_load = pltpu.make_async_copy(emb_hbm, emb, load.at[3])
    obs_load = pltpu.make_async_copy(obs_hbm, obs_raw, load.at[4])
    for copy in (w_loads[0], emb_load, *w_loads[1:], obs_load):
        copy.start()

    def at(x_, y_, z_):
        return ((x_ % 2) * RING + y_, ((x_ // 2) * RING + z_) * 2 + core)

    barrier = pltpu.get_barrier_semaphore()

    def greet(device):
        pl.semaphore_signal(barrier, inc=1, device_id=device, device_id_type=MESH)

    def member(j):
        return ((x_lo + 1 - j % 2) % 2) * RING + (y + far(j // 2, RING)) % RING

    def ring_a(p):
        return at(x, y + (1 - core) * (p - y), z + core * (p - z))

    def ring_b(p):
        return at(x, y + core * (p - y), z + (1 - core) * (p - z))

    def ring_x(p):
        return at(p, y, z)

    pos_a = y + core * (z - y)
    pos_b = z + core * (y - z)

    greet(other)
    greet(twin)

    @steps(0, MEMBERS - 1)
    def _(j):
        greet((member(j), row))

    @steps(0, RING - 1)
    def _(i):
        greet(at(x, y, (z + far(i, RING)) % RING))

    greet(at((x + 2) % 4, y, z))
    greet(at((x + 2) % 4 + 1 - 2 * (x % 2), y, z))
    greetings = MEMBERS - 1 + RING - 1 + 4

    for t in range(9):
        wp[t, 96:, :] = jnp.zeros((LANES - 96, LATENT), BF16)
    fbuf[LON:LON + 16, :] = jnp.zeros((16, LANES), F32)
    obs[...] = jnp.zeros_like(obs)

    def pad(part):
        w_loads[part].wait()
        for i in range(3):
            wp[order[part] + i, 0:CH, :] = w_ref[order[part] + i]

    pad(0)
    emb_load.wait()

    latitude = math.pi * ((row.astype(F32) + 0.5) / NLAT - 0.5)
    east_west = 1.0 / (0.25 + jnp.cos(jnp.full((1, LANES), latitude, F32)))

    def product(first):
        mat = wp[pl.ds(first, 3)].reshape(3 * LANES, LATENT)
        out = lax.dot_general(emb[...], mat, (((1,), (1,)), ((), ())), preferred_element_type=F32)
        return (pltpu.roll(out[:, 0:LANES], 1, 0), out[:, LANES:2 * LANES],
                pltpu.roll(out[:, 2 * LANES:3 * LANES], LON - 1, 0))

    def h_copy(slot, k):
        return remote(ps.at[slot, k], pr.at[slot, k], h_send.at[slot, k], h_recv.at[slot, k], (other, twin)[slot])

    for slot in range(2):
        lower = (1 - core) if slot == 0 else core
        west, mid, east = product(6 * lower)
        pad(slot + 1)
        fbuf[0:LON, :] = west + mid + east
        for k in range(MEMBERS):
            ps[slot, k] = fbuf[BLOCK * k:BLOCK * k + SLOT, :].astype(BF16)
        if slot == 0:
            pl.semaphore_wait(barrier, greetings)

        @steps(0, MEMBERS)
        def _(j):
            h_copy(slot, member(j)).start()

    west, mid, east = product(3)
    fbuf[0:LON, :] = mid + east_west * (west + east)
    for k in range(MEMBERS):
        pown[k] = fbuf[BLOCK * k:BLOCK * k + SLOT, :]

    def a_copy(k, slot):
        return remote(send_a.at[k], recv_a.at[slot], a_send.at[k], a_recv.at[slot], (k, row))

    def forecast(k):
        h_copy(1, k).wait_recv()
        h_copy(0, k).wait_recv()
        total = pown[k] + pr[1, k].astype(F32)
        return (total + jnp.where(inner, pr[0, k].astype(F32), 0.0)).astype(BF16)

    @steps(0, MEMBERS - 1)
    def _(j):
        k = member(j)
        send_a[k] = forecast(k)
        a_copy(k, me).start()

    vals[me] = forecast(me).astype(F32)

    def e_copy(i):
        piece = pl.ds(PIECE * i, PIECE)
        return remote(emb.at[piece], halo.at[piece], e_send.at[i], e_recv.at[i], twin)

    for i in range(PIECES):
        e_copy(i).start()

    obs_load.wait()
    for i in range(BLOCK):
        obs[i:i + 1, 0:CH] = obs_raw[i]

    @steps(0, MEMBERS - 1)
    def _(j):
        k = member(MEMBERS - 2 - j)
        a_copy(k, k).wait_recv()
        vals[k] = recv_a[k].astype(F32)

    area = area_ref[0]

    def score(j, loss):
        rows = pl.ds(pl.multiple_of(8 * j, 8), 8)
        f = [vals[i, rows, :] for i in range(MEMBERS)]
        o = obs[rows, :]
        grad, pair, total = [], [None] * MEMBERS, None
        pairs = None
        for i in range(MEMBERS):
            d = f[i] - o
            q = d * d + SMOOTHING
            r = lax.rsqrt(q)
            grad.append(d * r)
            total = q * r if total is None else total + q * r
        for i in range(MEMBERS):
            for k in range(i + 1, MEMBERS):
                d = f[i] - f[k]
                q = d * d + SMOOTHING
                r = lax.rsqrt(q)
                u = d * r
                pair[i] = u if pair[i] is None else pair[i] + u
                pair[k] = -u if pair[k] is None else pair[k] - u
                pairs = q * r if pairs is None else pairs + q * r
        for i in range(MEMBERS):
            vals[i, rows, :] = area * (grad[i] - PAIR_COEF * pair[i])
        crps = total - 0.5 * PAIR_COEF * (2.0 * pairs + MEMBERS * math.sqrt(SMOOTHING))
        lon = 8 * j + lax.broadcasted_iota(jnp.int32, (8, LANES), 0)
        ch = lax.broadcasted_iota(jnp.int32, (8, LANES), 1)
        return loss + jnp.where((lon < BLOCK) & (ch < CH), crps, 0.0)

    loss = lax.fori_loop(0, SLOT // 8, score, jnp.zeros((8, LANES), F32))

    def b_copy(k, slot):
        return remote(send_b.at[k], recv_b.at[slot], b_send.at[k], b_recv.at[slot], (k, row))

    @steps(0, MEMBERS - 1)
    def _(j):
        k = member(j)
        send_b[k] = vals[k].astype(BF16)
        b_copy(k, me).start()

    recv_b[me] = vals[me].astype(BF16)

    loss = area * jnp.sum(loss)
    sub = lax.broadcasted_iota(jnp.int32, (16, HALF), 0)
    lead = jnp.full((16, HALF), loss, F32).astype(BF16).astype(F32)
    tail = jnp.where(sub == 0, lead, jnp.where(sub == 1, loss - lead, 0.0))
    dw0[4 * CH:SUM_ROWS - 16, :] = jnp.zeros((SUM_ROWS - 16 - 4 * CH, HALF), F32)
    dw0[SUM_ROWS - 16:, :] = tail
    dw1[5 * CH:, :] = jnp.zeros((SUM_ROWS - 5 * CH, HALF), F32)
    for h in range(2):
        mid_sum[h, 3 * CH:, :] = jnp.zeros((MID_ROWS - 3 * CH, HALF), F32)

    def g_copy(slot, k, device):
        return remote(recv_b.at[k], hr.at[slot, k], g_send.at[slot, k], g_recv.at[slot, k], device)

    g_copy(0, me, other).start()
    g_copy(1, me, twin).start()

    @steps(0, MEMBERS - 1)
    def _(j):
        k = member(MEMBERS - 2 - j)
        b_copy(k, k).wait_recv()
        g_copy(0, k, other).start()
        g_copy(1, k, twin).start()

    def gather(slot, columns, block):
        for k in range(MEMBERS):
            gf[slot, 8 + BLOCK * k:8 + BLOCK * k + SLOT, :] = block(k).astype(F32)
        gf[slot, 7:8, :] = gf[slot, LON + 7:LON + 8, :]
        gf[slot, LON + 8:LON + 9, :] = gf[slot, 8:9, :]
        for b, column in enumerate(columns):
            gcat[:, column * LANES:(column + 1) * LANES] = gf[slot, 9 - b:9 - b + LON, :].astype(BF16)

    def arrive(slot):
        @steps(0, MEMBERS)
        def _(k):
            g_copy(slot, k, twin).wait_recv()

    def outer(column, latent):
        return lax.dot_general(gcat[:, column * LANES:(column + 3) * LANES], latent, (((0,), (0,)), ((), ())),
                               preferred_element_type=F32)

    def part(out, i, h):
        return out[LANES * i:LANES * i + CH, HALF * h:HALF * (h + 1)]

    flows = (
        Flow(SHAPES[0], (x, pos_a), (ring_x, ring_a), True, dw0, bufs[0], sums[0]),
        Flow(SHAPES[1], (pos_a, x), (ring_a, ring_x), False, dw1, bufs[1], sums[1]),
    )

    gather(0, (7, 6, 8), lambda k: recv_b[k])
    out = outer(6, emb[...])
    for i in range(3):
        for h in range(2):
            scale = 1.0 if i == 0 else east_west[:, 0:1]
            mid_sum[h, CH * i:CH * (i + 1), :] = part(out, i, h) * scale
    send_c[...] = mid_sum[1 - core].astype(BF16)
    c_copy = remote(send_c, recv_c, c_sem.at[0], c_sem.at[1], twin)
    c_copy.start()
    for i in range(PIECES):
        e_copy(i).wait_recv()
    with_twin = outer(6, halo[...])
    arrive(0)
    gather(1, (0, 1, 2), lambda k: jnp.where(inner, hr[0, k].astype(F32), 0.0))
    across = outer(0, emb[...])
    for group, base in ((1, 0), (0, 3)):
        for n, (b, h) in enumerate(UNITS[group]):
            rows = slice(CH * (base + n), CH * (base + n + 1))
            (dw0, dw1)[group][rows, :] = part(with_twin, (1, 0, 2)[b], h) + part(across, b, h)
    flows[1].step1()
    c_copy.wait_recv()
    dw0[0:3 * CH, :] = (mid_sum[core] + recv_c[...].astype(F32))[0:3 * CH]
    flows[0].step1()

    arrive(1)
    gather(2, (3, 4, 5), lambda k: hr[1, k])
    near = [wp[pl.ds(6 * first, 3)].reshape(3 * LANES, LATENT) for first in (1 - core, core)]
    plain = jnp.concatenate(near + [wp[4]], axis=0)
    scaled = jnp.concatenate([wp[3], wp[5]], axis=0)
    moved = jnp.dot(gcat[:, 0:7 * LANES], plain, preferred_element_type=F32)
    moved_ew = jnp.dot(gcat[:, 7 * LANES:], scaled, preferred_element_type=F32)
    d_ref[...] = (moved + east_west[:, 0:1] * moved_ew).astype(BF16)

    for flow in flows:
        flow.step2()
    for g, flow in enumerate(flows):
        s3[g] = flow.step3()

    def s3_copy(p, slot):
        return remote(s3, r3.at[slot], s3_send.at[p], s3_recv.at[slot], ring_b(p))

    @steps(0, RING - 1)
    def _(i):
        s3_copy((pos_b + far(i, RING)) % RING, pos_b).start()

    r3[pos_b] = s3[...]

    c_copy.wait_send()
    for i in range(PIECES):
        e_copy(i).wait_send()

    @steps(0, MEMBERS)
    def _(k):
        for slot in range(2):
            h_copy(slot, k).wait_send()
            g_copy(slot, k, twin).wait_send()

    @steps(0, MEMBERS - 1)
    def _(j):
        k = member(j)
        a_copy(k, me).wait_send()
        b_copy(k, me).wait_send()

    for flow in flows:
        flow.finish()

    @steps(0, RING - 1)
    def _(i):
        p = (pos_b + far(RING - 2 - i, RING)) % RING
        s3_copy(p, p).wait_recv()

    total = r3[0].astype(F32)
    for p in range(1, RING):
        total = total + r3[p].astype(F32)
    red[core, x, pos_a, 0] = flows[0].special(total[0]).astype(BF16)
    red[core, x, pos_a, 1] = total[1].astype(BF16)

    def ta_copy(i, slot):
        block = red.at[core, x, slot]
        return remote(block, block, ta_send.at[i], t_recv.at[x, slot], ring_a((pos_a + far(i, RING)) % RING))

    def tx_copy(i, x_, slot):
        block = red.at[core, x_, slot]
        return remote(block, block, tx_send.at[slot, i], t_recv.at[x_, slot], ring_x((x + far(i, 4)) % 4))

    def tc_copy(half, x_):
        block = red.at[half, x_]
        return remote(block, block, tc_send.at[x_], tc_recv.at[x_], twin)

    @steps(0, RING - 1)
    def _(i):
        ta_copy(i, pos_a).start()

    def along_x(slot):
        for i in range(3):
            tx_copy(i, x, slot).start()

    along_x(pos_a)

    @steps(0, RING - 1)
    def _(j):
        a_ = (pos_a + far(RING - 2 - j, RING)) % RING
        ta_copy(j, a_).wait_recv()
        along_x(a_)

    tc_copy(core, x).start()

    @steps(0, RING - 1)
    def _(i):
        s3_copy((pos_b + far(i, RING)) % RING, pos_b).wait_send()
        ta_copy(i, pos_a).wait_send()

    @steps(0, 3)
    def _(i):
        x_ = (x + far(2 - i, 4)) % 4
        for j in range(RING):
            tx_copy(i, x_, j).wait_recv()
        tc_copy(core, x_).start()

    @steps(0, RING)
    def _(slot):
        for i in range(3):
            tx_copy(i, x, slot).wait_send()

    @steps(0, 4)
    def _(x_):
        tc_copy(1 - core, x_).wait_recv()

    @steps(0, 4)
    def _(x_):
        tc_copy(core, x_).wait_send()


def unpack(d_ref, red, loss_ref, d_hbm, dw_hbm, buf, out, sem):
    move = pltpu.make_async_copy(d_ref, d_hbm, sem.at[9])
    move.start()
    for h in range(2):
        for x_ in range(4):
            for a_ in range(RING):
                for g, block in enumerate((x_ * RING + a_, a_ * 4 + x_)):
                    buf[g, h, 16 * block:16 * (block + 1), :] = red[h, x_, a_, g].astype(F32)
    tails = buf[0, :, SUM_ROWS - 16:SUM_ROWS - 14, 0:1]
    loss_ref[0] = jnp.sum(tails) * (1.0 / TALLY)

    def unit(t, h, g, core, i):
        out[t, :, HALF * h:HALF * (h + 1)] = buf[g, core, CH * i:CH * (i + 1), :] * (1.0 / TALLY)

    copies = []

    def leave(t):
        copies.append(pltpu.make_async_copy(out.at[t], dw_hbm.at[t], sem.at[t]))
        copies[-1].start()

    for i, t in enumerate(MIDDLE):
        for h in range(2):
            unit(t, h, 0, h, i)
        leave(t)
    for core in range(2):
        for b in range(3):
            for h in range(2):
                group = 0 if (b, h) in UNITS[0] else 1
                unit(6 * (1 - core) + b, h, group, core, (3, 0)[group] + UNITS[group].index((b, h)))
            leave(6 * (1 - core) + b)
    for copy in copies:
        copy.wait()
    move.wait()


def per_device(member_embedding, weights, verifying_observed_grid, area_weight):
    emb = member_embedding[0, :, 0, :].T
    obs = jnp.transpose(verifying_observed_grid, (2, 1, 0))
    vmem = pl.BlockSpec(memory_space=pltpu.VMEM)
    smem = pl.BlockSpec(memory_space=pltpu.SMEM)
    hbm = pl.BlockSpec(memory_space=pltpu.HBM)
    dma = lambda *n: pltpu.SemaphoreType.DMA(n)
    blocks = lambda kind: pltpu.VMEM((MEMBERS, SLOT, LANES), kind)
    scratch = [
        pltpu.VMEM((LON, LATENT), BF16),
        pltpu.VMEM((LON, LATENT), BF16),
        pltpu.VMEM((9, CH, LATENT), BF16),
        pltpu.VMEM((BLOCK, 1, CH), F32),
        pltpu.VMEM((SLOT, LANES), F32),
        pltpu.VMEM((9, LANES, LATENT), BF16),
        pltpu.VMEM((LON + 16, LANES), F32),
        blocks(F32),
        pltpu.VMEM((2, MEMBERS, SLOT, LANES), BF16),
        pltpu.VMEM((2, MEMBERS, SLOT, LANES), BF16),
        blocks(BF16),
        blocks(BF16),
        blocks(F32),
        blocks(BF16),
        blocks(BF16),
        pltpu.VMEM((2, MEMBERS, SLOT, LANES), BF16),
        pltpu.VMEM((3, LON + 32, LANES), F32),
        pltpu.VMEM((LON, 9 * LANES), BF16),
        pltpu.VMEM((2, MID_ROWS, HALF), F32),
        pltpu.VMEM((MID_ROWS, HALF), BF16),
        pltpu.VMEM((MID_ROWS, HALF), BF16),
        pltpu.VMEM((SUM_ROWS, HALF), F32),
        pltpu.VMEM((SUM_ROWS, HALF), F32),
        pltpu.VMEM((2, 16, HALF), BF16),
        pltpu.VMEM((RING, 2, 16, HALF), BF16),
    ]
    for first, second in SHAPES:
        big = pltpu.VMEM((first, 16 * second, HALF), BF16)
        small = pltpu.VMEM((second, 16, HALF), BF16)
        scratch += [big, big, small, small]
    scratch += [dma(5), dma(2, MEMBERS), dma(2, MEMBERS), dma(PIECES), dma(PIECES),
                dma(MEMBERS), dma(MEMBERS), dma(MEMBERS), dma(MEMBERS), dma(2, MEMBERS), dma(2, MEMBERS), dma(2),
                dma(RING), dma(RING), dma(RING), dma(RING, 3), dma(4, RING), dma(4), dma(4)]
    for first, second in SHAPES:
        for size in (first, second):
            scratch += [dma(size), dma(size)]
    moved, red = pl.pallas_call(
        kernel,
        out_shape=(jax.ShapeDtypeStruct((LON, LATENT), BF16),
                   jax.ShapeDtypeStruct((2, 4, RING, 2, 16, HALF), BF16)),
        in_specs=[smem, hbm, hbm, hbm],
        out_specs=(vmem, vmem),
        scratch_shapes=scratch,
        compiler_params=pltpu.CompilerParams(
            collective_id=0, has_side_effects=True, vmem_limit_bytes=48 * 1024 * 1024),
        cost_estimate=pl.CostEstimate(flops=2_600_000_000, bytes_accessed=6_000_000, transcendentals=1_000_000),
        name="decoder",
    )(area_weight, *(pltpu.with_memory_space_constraint(a, pltpu.HBM) for a in (emb, weights, obs)))
    loss, moved, grad_weight = pl.pallas_call(
        unpack,
        out_shape=(jax.ShapeDtypeStruct((1,), F32), jax.ShapeDtypeStruct((LON, LATENT), BF16),
                   jax.ShapeDtypeStruct((9, CH, LATENT), F32)),
        in_specs=[vmem, vmem],
        out_specs=(smem, hbm, hbm),
        scratch_shapes=[pltpu.VMEM((2, 2, SUM_ROWS, HALF), F32), pltpu.VMEM((9, CH, LATENT), F32), dma(10)],
        compiler_params=pltpu.CompilerParams(vmem_limit_bytes=32 * 1024 * 1024),
        cost_estimate=pl.CostEstimate(flops=1_000_000, bytes_accessed=4_500_000, transcendentals=0),
        name="unpack",
    )(moved, red)
    return loss.reshape(()), moved.T[None, :, None, :], grad_weight


def solution(mesh):
    return jax.shard_map(
        per_device,
        mesh=mesh,
        in_specs=(P("ens", None, "space", None), P(), P(None, "space", "ens"), P("space")),
        out_specs=(P(), P("ens", None, "space", None), P()),
        check_vma=False,
    )
```

```python
import math

import jax
import jax.numpy as jnp
from jax import lax
from jax.experimental import pallas as pl
from jax.experimental.pallas import tpu as pltpu
from jax.sharding import PartitionSpec as P

MESH = pl.DeviceIdType.MESH
F32 = jnp.float32
BF16 = jnp.bfloat16

CH, LATENT, LON, MEMBERS, NLAT = 100, 512, 720, 16, 32
LANES = 128
BLOCK = LON // MEMBERS
SLOT = 48
RING = 8
HALF = LATENT // 2
SUM_ROWS = 512
SMOOTHING = 0.01
PAIR_COEF = (1.0 - 0.05 / MEMBERS) / (MEMBERS - 1)
TALLY = MEMBERS * NLAT * LON
MIDDLE = (4, 3, 5)
UNITS = (((0, 0),), ((0, 1), (1, 0), (1, 1), (2, 0), (2, 1)))
MID_ROWS = 304
SHAPES = ((4, 8), (8, 4))


def steps(first, end):
    return pl.loop(first, end, unroll=True)


def remote(src, dst, send_sem, recv_sem, device):
    return pltpu.make_async_remote_copy(
        src_ref=src, dst_ref=dst, send_sem=send_sem, recv_sem=recv_sem,
        device_id=device, device_id_type=MESH,
    )


def mod(a, n):
    return a % n if isinstance(a, int) else lax.rem(a, jnp.int32(n))


def over(a, n):
    return a // n if isinstance(a, int) else lax.div(a, jnp.int32(n))


def far(i, size):
    odd = mod(i, 2)
    return size // 2 + over(i, 2) * (1 - odd) - over(i + 1, 2) * odd


def resplit(block):
    total = block[0:1] + block[1:2]
    lead = total.astype(BF16).astype(F32)
    row = lax.broadcasted_iota(jnp.int32, block.shape, 0)
    return jnp.where(row == 0, lead, jnp.where(row == 1, total - lead, block))


class Flow:
    def __init__(self, shape, pos, rings, has_loss, dw, bufs, sems):
        self.first, self.second = shape
        self.pos, self.rings = pos, rings
        self.has_loss = has_loss
        self.dw = dw
        self.s1, self.r1, self.s2, self.r2 = bufs
        self.sems = sems
        self.rows = 16 * self.second

    def copy(self, phase, src, dst, send, recv, device):
        return remote(src, dst, self.sems[2 * phase].at[send], self.sems[2 * phase + 1].at[recv], device)

    def s1_copy(self, p, slot):
        return self.copy(0, self.s1.at[p], self.r1.at[slot], p, slot, self.rings[0](p))

    def s2_copy(self, p, slot):
        return self.copy(1, self.s2.at[p], self.r2.at[slot], p, slot, self.rings[1](p))

    def peers(self, ring, body, near=False):
        size = (self.first, self.second)[ring]

        @steps(0, size - 1)
        def _(i):
            body(mod(self.pos[ring] + far(size - 2 - i if near else i, size), size))

    def step1(self):
        for p in range(self.first):
            self.s1[p] = self.dw[p * self.rows:(p + 1) * self.rows, :].astype(BF16)
        self.peers(0, lambda p: self.s1_copy(p, self.pos[0]).start())
        self.r1[self.pos[0]] = self.s1[self.pos[0]]

    def step2(self):
        self.peers(0, lambda p: self.s1_copy(p, p).wait_recv(), near=True)
        total = self.r1[0].astype(F32)
        for p in range(1, self.first):
            total = total + self.r1[p].astype(F32)
        for q in range(self.second):
            block = total[16 * q:16 * (q + 1)]
            if self.has_loss and q == self.second - 1:
                block = jnp.where(self.pos[0] == self.first - 1, resplit(block), block)
            self.s2[q] = block.astype(BF16)
        self.peers(1, lambda p: self.s2_copy(p, self.pos[1]).start())
        self.r2[self.pos[1]] = self.s2[self.pos[1]]

    def special(self, block):
        if not self.has_loss:
            return block
        here = (self.pos[0] == self.first - 1) & (self.pos[1] == self.second - 1)
        return jnp.where(here, resplit(block), block)

    def step3(self):
        self.peers(1, lambda p: self.s2_copy(p, p).wait_recv(), near=True)
        total = self.r2[0].astype(F32)
        for p in range(1, self.second):
            total = total + self.r2[p].astype(F32)
        return self.special(total).astype(BF16)

    def finish(self):
        self.peers(0, lambda p: self.s1_copy(p, self.pos[0]).wait_send())
        self.peers(1, lambda p: self.s2_copy(p, self.pos[1]).wait_send())


def kernel(area_ref, emb_hbm, w_hbm, obs_hbm, d_ref, red, *scratch):
    (emb, halo, w_ref, obs_raw, obs, wp, fbuf, pown, ps, pr, send_a, recv_a, vals, send_b, recv_b, hr, gf, gcat,
     mid_sum, send_c, recv_c, dw0, dw1) = scratch[:23]
    s3, r3, waits = scratch[23:26]
    bufs = (scratch[26:30], scratch[30:34])
    (load, h_send, h_recv, e_sem, a_send, a_recv, b_send, b_recv, g_send, g_recv, c_sem,
     s3_send, s3_recv, t_send, t_recv, tc_send, tc_recv) = scratch[34:51]
    sums = (scratch[51:55], scratch[55:59])

    me = lax.axis_index("ens")
    row = lax.axis_index("space")
    x_lo, y = over(me, RING), mod(me, RING)
    core = mod(row, 2)
    z = mod(over(row, 2), RING)
    x_hi = over(row, 2 * RING)
    x = 2 * x_hi + x_lo
    twin = (me, row + 1 - 2 * core)
    next_row = mod(row + 2 * core - 1 + NLAT, NLAT)
    other = (me, next_row)
    inner = (row > 0) & (row < NLAT - 1)

    order = [3 * mod(2 * (1 - core) + i * (1 + core), 3) for i in range(3)]
    w_loads = [pltpu.make_async_copy(w_hbm.at[pl.ds(t, 3)], w_ref.at[pl.ds(t, 3)], load.at[i])
               for i, t in enumerate(order)]
    emb_load = pltpu.make_async_copy(emb_hbm, emb, load.at[3])
    obs_load = pltpu.make_async_copy(obs_hbm, obs_raw, load.at[4])
    for copy in (w_loads[0], emb_load, *w_loads[1:], obs_load):
        copy.start()

    def at(x_, y_, z_):
        return (mod(x_, 2) * RING + y_, (over(x_, 2) * RING + z_) * 2 + core)

    barrier = pltpu.get_barrier_semaphore()

    def greet(device):
        pl.semaphore_signal(barrier, inc=1, device_id=device, device_id_type=MESH)

    def member(j):
        return mod(x_lo + 1 - mod(j, 2), 2) * RING + mod(y + far(over(j, 2), RING), RING)

    def ring_a(p):
        return at(x, y + (1 - core) * (p - y), z + core * (p - z))

    def ring_b(p):
        return at(x, y + core * (p - y), z + (1 - core) * (p - z))

    def ring_x(p):
        return at(p, y, z)

    pos_a = y + core * (z - y)
    pos_b = z + core * (y - z)

    greet(other)
    greet(twin)

    @steps(0, MEMBERS - 1)
    def _(j):
        greet((member(j), row))

    @steps(0, RING - 1)
    def _(i):
        greet(at(x, y, mod(z + far(i, RING), RING)))

    greet(at(mod(x + 2, 4), y, z))
    greet(at(mod(x + 2, 4) + 1 - 2 * mod(x, 2), y, z))
    greetings = MEMBERS - 1 + RING - 1 + 4

    for t in range(9):
        wp[t, 96:, :] = jnp.zeros((LANES - 96, LATENT), BF16)
    fbuf[LON:LON + 16, :] = jnp.zeros((16, LANES), F32)
    obs[...] = jnp.zeros_like(obs)

    def pad(part):
        w_loads[part].wait()
        for i in range(3):
            wp[order[part] + i, 0:CH, :] = w_ref[order[part] + i]

    pad(0)
    emb_load.wait()

    latitude = math.pi * ((row.astype(F32) + 0.5) / NLAT - 0.5)
    east_west = 1.0 / (0.25 + jnp.cos(jnp.full((1, LANES), latitude, F32)))

    def product(first):
        mat = wp[pl.ds(first, 3)].reshape(3 * LANES, LATENT)
        out = lax.dot_general(emb[...], mat, (((1,), (1,)), ((), ())), preferred_element_type=F32)
        return (pltpu.roll(out[:, 0:LANES], 1, 0), out[:, LANES:2 * LANES],
                pltpu.roll(out[:, 2 * LANES:3 * LANES], LON - 1, 0))

    def h_copy(k):
        return remote(ps.at[0, k], pr.at[0, k], h_send.at[k], h_recv.at[k], other)

    h_twin = remote(ps.at[1], pr.at[1], h_send.at[MEMBERS], h_recv.at[MEMBERS], twin)

    for slot in range(2):
        lower = (1 - core) if slot == 0 else core
        west, mid, east = product(6 * lower)
        pad(slot + 1)
        fbuf[0:LON, :] = west + mid + east
        for k in range(MEMBERS):
            ps[slot, k] = fbuf[BLOCK * k:BLOCK * k + SLOT, :].astype(BF16)
        if slot == 1:
            h_twin.start()
            continue
        pl.semaphore_wait(barrier, greetings)

        @steps(0, MEMBERS)
        def _(j):
            h_copy(member(j)).start()

    west, mid, east = product(3)
    fbuf[0:LON, :] = mid + east_west * (west + east)
    for k in range(MEMBERS):
        pown[k] = fbuf[BLOCK * k:BLOCK * k + SLOT, :]

    def a_copy(k, slot):
        return remote(send_a.at[k], recv_a.at[slot], a_send.at[k], a_recv.at[slot], (k, row))

    def forecast(k):
        h_copy(k).wait_recv()
        total = pown[k] + pr[1, k].astype(F32)
        return (total + jnp.where(inner, pr[0, k].astype(F32), 0.0)).astype(BF16)

    h_twin.wait_recv()

    @steps(0, MEMBERS - 1)
    def _(j):
        k = member(j)
        send_a[k] = forecast(k)
        a_copy(k, me).start()

    vals[me] = forecast(me).astype(F32)

    e_copy = remote(emb, halo, e_sem.at[0], e_sem.at[1], twin)
    e_copy.start()

    obs_load.wait()
    for i in range(BLOCK):
        obs[i:i + 1, 0:CH] = obs_raw[i]

    @steps(0, MEMBERS - 1)
    def _(j):
        k = member(MEMBERS - 2 - j)
        a_copy(k, k).wait_recv()
        vals[k] = recv_a[k].astype(F32)

    area = area_ref[0]

    def score(j, loss):
        rows = pl.ds(pl.multiple_of(8 * j, 8), 8)
        f = [vals[i, rows, :] for i in range(MEMBERS)]
        o = obs[rows, :]
        grad, pair, total = [], [None] * MEMBERS, None
        pairs = None
        for i in range(MEMBERS):
            d = f[i] - o
            q = d * d + SMOOTHING
            r = lax.rsqrt(q)
            grad.append(d * r)
            total = q * r if total is None else total + q * r
        for i in range(MEMBERS):
            for k in range(i + 1, MEMBERS):
                d = f[i] - f[k]
                q = d * d + SMOOTHING
                r = lax.rsqrt(q)
                u = d * r
                pair[i] = u if pair[i] is None else pair[i] + u
                pair[k] = -u if pair[k] is None else pair[k] - u
                pairs = q * r if pairs is None else pairs + q * r
        for i in range(MEMBERS):
            vals[i, rows, :] = area * (grad[i] - PAIR_COEF * pair[i])
        crps = total - 0.5 * PAIR_COEF * (2.0 * pairs + MEMBERS * math.sqrt(SMOOTHING))
        lon = 8 * j + lax.broadcasted_iota(jnp.int32, (8, LANES), 0)
        ch = lax.broadcasted_iota(jnp.int32, (8, LANES), 1)
        return loss + jnp.where((lon < BLOCK) & (ch < CH), crps, 0.0)

    loss = lax.fori_loop(0, SLOT // 8, score, jnp.zeros((8, LANES), F32))

    def b_copy(k, slot):
        return remote(send_b.at[k], recv_b.at[slot], b_send.at[k], b_recv.at[slot], (k, row))

    @steps(0, MEMBERS - 1)
    def _(j):
        k = member(j)
        send_b[k] = vals[k].astype(BF16)
        b_copy(k, me).start()

    recv_b[me] = vals[me].astype(BF16)

    loss = area * jnp.sum(loss)
    sub = lax.broadcasted_iota(jnp.int32, (16, HALF), 0)
    lead = jnp.full((16, HALF), loss, F32).astype(BF16).astype(F32)
    tail = jnp.where(sub == 0, lead, jnp.where(sub == 1, loss - lead, 0.0))
    dw0[4 * CH:SUM_ROWS - 16, :] = jnp.zeros((SUM_ROWS - 16 - 4 * CH, HALF), F32)
    dw0[SUM_ROWS - 16:, :] = tail
    dw1[5 * CH:, :] = jnp.zeros((SUM_ROWS - 5 * CH, HALF), F32)
    for h in range(2):
        mid_sum[h, 3 * CH:, :] = jnp.zeros((MID_ROWS - 3 * CH, HALF), F32)

    def g_copy(k):
        return remote(recv_b.at[k], hr.at[0, k], g_send.at[k], g_recv.at[k], other)

    g_copy(me).start()

    @steps(0, MEMBERS - 1)
    def _(j):
        k = member(MEMBERS - 2 - j)
        b_copy(k, k).wait_recv()
        g_copy(k).start()

    g_twin = remote(recv_b, hr.at[1], g_send.at[MEMBERS], g_recv.at[MEMBERS], twin)
    g_twin.start()

    def gather(slot, columns, block):
        for k in range(MEMBERS):
            gf[slot, 8 + BLOCK * k:8 + BLOCK * k + SLOT, :] = block(k).astype(F32)
        gf[slot, 7:8, :] = gf[slot, LON + 7:LON + 8, :]
        gf[slot, LON + 8:LON + 9, :] = gf[slot, 8:9, :]
        for b, column in enumerate(columns):
            gcat[:, column * LANES:(column + 1) * LANES] = gf[slot, 9 - b:9 - b + LON, :].astype(BF16)

    def outer(column, latent):
        return lax.dot_general(gcat[:, column * LANES:(column + 3) * LANES], latent, (((0,), (0,)), ((), ())),
                               preferred_element_type=F32)

    def part(out, i, h):
        return out[LANES * i:LANES * i + CH, HALF * h:HALF * (h + 1)]

    flows = (
        Flow(SHAPES[0], (x, pos_a), (ring_x, ring_a), True, dw0, bufs[0], sums[0]),
        Flow(SHAPES[1], (pos_a, x), (ring_a, ring_x), False, dw1, bufs[1], sums[1]),
    )

    gather(0, (7, 6, 8), lambda k: recv_b[k])
    out = outer(6, emb[...])
    for i in range(3):
        for h in range(2):
            scale = 1.0 if i == 0 else east_west[:, 0:1]
            mid_sum[h, CH * i:CH * (i + 1), :] = part(out, i, h) * scale
    send_c[...] = mid_sum[1 - core].astype(BF16)
    c_copy = remote(send_c, recv_c, c_sem.at[0], c_sem.at[1], twin)
    c_copy.start()
    e_copy.wait_recv()
    with_twin = outer(6, halo[...])

    @steps(0, MEMBERS)
    def _(k):
        g_copy(k).wait_recv()

    gather(1, (0, 1, 2), lambda k: jnp.where(inner, hr[0, k].astype(F32), 0.0))
    across = outer(0, emb[...])
    for group, base in ((1, 0), (0, 3)):
        for n, (b, h) in enumerate(UNITS[group]):
            rows = slice(CH * (base + n), CH * (base + n + 1))
            (dw0, dw1)[group][rows, :] = part(with_twin, (1, 0, 2)[b], h) + part(across, b, h)
    flows[1].step1()
    c_copy.wait_recv()
    dw0[0:3 * CH, :] = (mid_sum[core] + recv_c[...].astype(F32))[0:3 * CH]
    flows[0].step1()

    g_twin.wait_recv()
    gather(2, (3, 4, 5), lambda k: hr[1, k])
    near = [wp[pl.ds(6 * first, 3)].reshape(3 * LANES, LATENT) for first in (1 - core, core)]
    plain = jnp.concatenate(near + [wp[4]], axis=0)
    scaled = jnp.concatenate([wp[3], wp[5]], axis=0)
    moved = jnp.dot(gcat[:, 0:7 * LANES], plain, preferred_element_type=F32)
    moved_ew = jnp.dot(gcat[:, 7 * LANES:], scaled, preferred_element_type=F32)
    d_ref[...] = (moved + east_west[:, 0:1] * moved_ew).astype(BF16)

    for flow in flows:
        flow.step2()
    for g, flow in enumerate(flows):
        s3[g] = flow.step3()

    def s3_copy(p, slot):
        return remote(s3, r3.at[slot], s3_send.at[p], s3_recv.at[slot], ring_b(p))

    @steps(0, RING - 1)
    def _(i):
        s3_copy(mod(pos_b + far(i, RING), RING), pos_b).start()

    r3[pos_b] = s3[...]

    c_copy.wait_send()
    e_copy.wait_send()
    h_twin.wait_send()
    g_twin.wait_send()

    @steps(0, MEMBERS)
    def _(k):
        h_copy(k).wait_send()
        g_copy(k).wait_send()

    @steps(0, MEMBERS - 1)
    def _(j):
        k = member(j)
        a_copy(k, me).wait_send()
        b_copy(k, me).wait_send()

    for flow in flows:
        flow.finish()

    @steps(0, RING - 1)
    def _(i):
        p = mod(pos_b + far(RING - 2 - i, RING), RING)
        s3_copy(p, p).wait_recv()

    total = r3[0].astype(F32)
    for p in range(1, RING):
        total = total + r3[p].astype(F32)
    red[core, x, pos_a, 0] = flows[0].special(total[0]).astype(BF16)
    red[core, x, pos_a, 1] = total[1].astype(BF16)

    def ta_copy(g, x_, i):
        block = red.at[core, x_, pos_a, g]
        return remote(block, block, t_send.at[g], t_recv.at[x_, pos_a, g], ring_a(mod(pos_a + far(i, RING), RING)))

    def tx_copy(g, slot, i):
        block = red.at[core, x, slot, g]
        return remote(block, block, t_send.at[2 + g], t_recv.at[x, slot, g], ring_x(mod(x + far(i, 4), 4)))

    def along_x(g, slot):
        for i in range(3):
            tx_copy(g, slot, i).start()

    def along_ring(g, x_):
        for i in range(RING - 1):
            ta_copy(g, x_, i).start()

    def landed(x_, slot, g):
        block = red.at[core, x_, slot, g]
        remote(block, block, t_send.at[0], t_recv.at[x_, slot, g], twin).wait_recv()

    def left(sem, blocks, like):
        part = like.at[pl.ds(0, blocks)]
        pltpu.make_async_copy(part, part, t_send.at[sem]).wait()

    def tc_copy(half, x_):
        block = red.at[half, x_]
        return remote(block, block, tc_send.at[x_], tc_recv.at[x_], twin)

    along_x(1, pos_a)
    along_ring(0, x)
    along_x(0, pos_a)
    along_ring(1, x)

    def from_ring(*offsets):
        for offset in offsets:
            slot = mod(pos_a + offset, RING)
            landed(x, slot, 0)
            along_x(0, slot)

    def from_x(*offsets):
        for offset in offsets:
            x_ = mod(x + offset, 4)
            landed(x_, pos_a, 1)
            along_ring(1, x_)

    from_ring(1, 7)
    from_x(1, 3)
    from_ring(2, 6)
    from_x(2)
    from_ring(3, 5, 4)

    @steps(1, RING)
    def _(i):
        landed(x, mod(pos_a + i, RING), 1)

    tc_copy(core, x).start()

    @steps(0, RING - 1)
    def _(i):
        s3_copy(mod(pos_b + far(i, RING), RING), pos_b).wait_send()

    for offset in (1, 3, 2):
        x_ = mod(x + offset, 4)
        landed(x_, pos_a, 0)

        @steps(1, RING)
        def _(i):
            for g in range(2):
                landed(x_, mod(pos_a + i, RING), g)

        tc_copy(core, x_).start()

    left(0, RING - 1, flows[0].s2)
    left(1, 4 * (RING - 1), waits)
    left(2, 3 * RING, waits)
    left(3, 3, flows[0].s2)

    @steps(0, 4)
    def _(x_):
        tc_copy(1 - core, x_).wait_recv()

    @steps(0, 4)
    def _(x_):
        tc_copy(core, x_).wait_send()


def unpack(d_ref, red, loss_ref, d_hbm, dw_hbm, buf, out, sem):
    move = pltpu.make_async_copy(d_ref, d_hbm, sem.at[9])
    move.start()
    for h in range(2):
        for x_ in range(4):
            for a_ in range(RING):
                for g, block in enumerate((x_ * RING + a_, a_ * 4 + x_)):
                    buf[g, h, 16 * block:16 * (block + 1), :] = red[h, x_, a_, g].astype(F32)
    tails = buf[0, :, SUM_ROWS - 16:SUM_ROWS - 14, 0:1]
    loss_ref[0] = jnp.sum(tails) * (1.0 / TALLY)

    def unit(t, h, g, core, i):
        out[t, :, HALF * h:HALF * (h + 1)] = buf[g, core, CH * i:CH * (i + 1), :] * (1.0 / TALLY)

    copies = []

    def leave(t):
        copies.append(pltpu.make_async_copy(out.at[t], dw_hbm.at[t], sem.at[t]))
        copies[-1].start()

    for i, t in enumerate(MIDDLE):
        for h in range(2):
            unit(t, h, 0, h, i)
        leave(t)
    for core in range(2):
        for b in range(3):
            for h in range(2):
                group = 0 if (b, h) in UNITS[0] else 1
                unit(6 * (1 - core) + b, h, group, core, (3, 0)[group] + UNITS[group].index((b, h)))
            leave(6 * (1 - core) + b)
    for copy in copies:
        copy.wait()
    move.wait()


def per_device(member_embedding, weights, verifying_observed_grid, area_weight):
    emb = member_embedding[0, :, 0, :].T
    obs = jnp.transpose(verifying_observed_grid, (2, 1, 0))
    vmem = pl.BlockSpec(memory_space=pltpu.VMEM)
    smem = pl.BlockSpec(memory_space=pltpu.SMEM)
    hbm = pl.BlockSpec(memory_space=pltpu.HBM)
    dma = lambda *n: pltpu.SemaphoreType.DMA(n)
    blocks = lambda kind: pltpu.VMEM((MEMBERS, SLOT, LANES), kind)
    scratch = [
        pltpu.VMEM((LON, LATENT), BF16),
        pltpu.VMEM((LON, LATENT), BF16),
        pltpu.VMEM((9, CH, LATENT), BF16),
        pltpu.VMEM((BLOCK, 1, CH), F32),
        pltpu.VMEM((SLOT, LANES), F32),
        pltpu.VMEM((9, LANES, LATENT), BF16),
        pltpu.VMEM((LON + 16, LANES), F32),
        blocks(F32),
        pltpu.VMEM((2, MEMBERS, SLOT, LANES), BF16),
        pltpu.VMEM((2, MEMBERS, SLOT, LANES), BF16),
        blocks(BF16),
        blocks(BF16),
        blocks(F32),
        blocks(BF16),
        blocks(BF16),
        pltpu.VMEM((2, MEMBERS, SLOT, LANES), BF16),
        pltpu.VMEM((3, LON + 32, LANES), F32),
        pltpu.VMEM((LON, 9 * LANES), BF16),
        pltpu.VMEM((2, MID_ROWS, HALF), F32),
        pltpu.VMEM((MID_ROWS, HALF), BF16),
        pltpu.VMEM((MID_ROWS, HALF), BF16),
        pltpu.VMEM((SUM_ROWS, HALF), F32),
        pltpu.VMEM((SUM_ROWS, HALF), F32),
        pltpu.VMEM((2, 16, HALF), BF16),
        pltpu.VMEM((RING, 2, 16, HALF), BF16),
        pltpu.VMEM((4 * RING, 16, HALF), BF16),
    ]
    for first, second in SHAPES:
        big = pltpu.VMEM((first, 16 * second, HALF), BF16)
        small = pltpu.VMEM((second, 16, HALF), BF16)
        scratch += [big, big, small, small]
    scratch += [dma(5), dma(MEMBERS + 1), dma(MEMBERS + 1), dma(2),
                dma(MEMBERS), dma(MEMBERS), dma(MEMBERS), dma(MEMBERS), dma(MEMBERS + 1), dma(MEMBERS + 1), dma(2),
                dma(RING), dma(RING), dma(4), dma(4, RING, 2), dma(4), dma(4)]
    for first, second in SHAPES:
        for size in (first, second):
            scratch += [dma(size), dma(size)]
    moved, red = pl.pallas_call(
        kernel,
        out_shape=(jax.ShapeDtypeStruct((LON, LATENT), BF16),
                   jax.ShapeDtypeStruct((2, 4, RING, 2, 16, HALF), BF16)),
        in_specs=[smem, hbm, hbm, hbm],
        out_specs=(vmem, vmem),
        scratch_shapes=scratch,
        compiler_params=pltpu.CompilerParams(
            collective_id=0, has_side_effects=True, vmem_limit_bytes=48 * 1024 * 1024),
        cost_estimate=pl.CostEstimate(flops=2_600_000_000, bytes_accessed=6_000_000, transcendentals=1_000_000),
        name="decoder",
    )(area_weight, *(pltpu.with_memory_space_constraint(a, pltpu.HBM) for a in (emb, weights, obs)))
    loss, moved, grad_weight = pl.pallas_call(
        unpack,
        out_shape=(jax.ShapeDtypeStruct((1,), F32), jax.ShapeDtypeStruct((LON, LATENT), BF16),
                   jax.ShapeDtypeStruct((9, CH, LATENT), F32)),
        in_specs=[vmem, vmem],
        out_specs=(smem, hbm, hbm),
        scratch_shapes=[pltpu.VMEM((2, 2, SUM_ROWS, HALF), F32), pltpu.VMEM((9, CH, LATENT), F32), dma(10)],
        compiler_params=pltpu.CompilerParams(vmem_limit_bytes=32 * 1024 * 1024),
        cost_estimate=pl.CostEstimate(flops=1_000_000, bytes_accessed=4_500_000, transcendentals=0),
        name="unpack",
    )(moved, red)
    return loss.reshape(()), moved.T[None, :, None, :], grad_weight


def solution(mesh):
    return jax.shard_map(
        per_device,
        mesh=mesh,
        in_specs=(P("ens", None, "space", None), P(), P(None, "space", "ens"), P("space")),
        out_specs=(P(), P("ens", None, "space", None), P()),
        check_vma=False,
    )
```

```python
import math

import jax
import jax.numpy as jnp
from jax import lax
from jax.experimental import pallas as pl
from jax.experimental.pallas import tpu as pltpu
from jax.sharding import PartitionSpec as P

MESH = pl.DeviceIdType.MESH
F32 = jnp.float32
BF16 = jnp.bfloat16

CH, LATENT, LON, MEMBERS, NLAT = 100, 512, 720, 16, 32
LANES = 128
BLOCK = LON // MEMBERS
SLOT = 48
RING = 8
HALF = LATENT // 2
SUM_ROWS = 512
SMOOTHING = 0.01
PAIR_COEF = (1.0 - 0.05 / MEMBERS) / (MEMBERS - 1)
TALLY = MEMBERS * NLAT * LON
MIDDLE = (4, 3, 5)
UNITS = (((0, 0),), ((0, 1), (1, 0), (1, 1), (2, 0), (2, 1)))
MID_ROWS = 304
SHAPES = ((4, 8), (8, 4))


def steps(first, end):
    return pl.loop(first, end, unroll=True)


def remote(src, dst, send_sem, recv_sem, device):
    return pltpu.make_async_remote_copy(
        src_ref=src, dst_ref=dst, send_sem=send_sem, recv_sem=recv_sem,
        device_id=device, device_id_type=MESH,
    )


def mod(a, n):
    return a % n if isinstance(a, int) else lax.rem(a, jnp.int32(n))


def over(a, n):
    return a // n if isinstance(a, int) else lax.div(a, jnp.int32(n))


def far(i, size):
    odd = mod(i, 2)
    return size // 2 + over(i, 2) * (1 - odd) - over(i + 1, 2) * odd


def resplit(block):
    total = block[0:1] + block[1:2]
    lead = total.astype(BF16).astype(F32)
    row = lax.broadcasted_iota(jnp.int32, block.shape, 0)
    return jnp.where(row == 0, lead, jnp.where(row == 1, total - lead, block))


class Flow:
    def __init__(self, shape, pos, rings, has_loss, dw, bufs, sems):
        self.first, self.second = shape
        self.pos, self.rings = pos, rings
        self.has_loss = has_loss
        self.dw = dw
        self.s1, self.r1, self.s2, self.r2 = bufs
        self.sems = sems
        self.rows = 16 * self.second

    def copy(self, phase, src, dst, send, recv, device):
        return remote(src, dst, self.sems[2 * phase].at[send], self.sems[2 * phase + 1].at[recv], device)

    def s1_copy(self, p, slot):
        return self.copy(0, self.s1.at[p], self.r1.at[slot], p, slot, self.rings[0](p))

    def s2_copy(self, p, slot):
        return self.copy(1, self.s2.at[p], self.r2.at[slot], p, slot, self.rings[1](p))

    def peers(self, ring, body, near=False):
        size = (self.first, self.second)[ring]

        @steps(0, size - 1)
        def _(i):
            body(mod(self.pos[ring] + far(size - 2 - i if near else i, size), size))

    def step1(self):
        for p in range(self.first):
            self.s1[p] = self.dw[p * self.rows:(p + 1) * self.rows, :].astype(BF16)
        self.peers(0, lambda p: self.s1_copy(p, self.pos[0]).start())
        self.r1[self.pos[0]] = self.s1[self.pos[0]]

    def step2(self):
        self.peers(0, lambda p: self.s1_copy(p, p).wait_recv(), near=True)
        total = self.r1[0].astype(F32)
        for p in range(1, self.first):
            total = total + self.r1[p].astype(F32)
        for q in range(self.second):
            block = total[16 * q:16 * (q + 1)]
            if self.has_loss and q == self.second - 1:
                block = jnp.where(self.pos[0] == self.first - 1, resplit(block), block)
            self.s2[q] = block.astype(BF16)
        self.peers(1, lambda p: self.s2_copy(p, self.pos[1]).start())
        self.r2[self.pos[1]] = self.s2[self.pos[1]]

    def special(self, block):
        if not self.has_loss:
            return block
        here = (self.pos[0] == self.first - 1) & (self.pos[1] == self.second - 1)
        return jnp.where(here, resplit(block), block)

    def step3(self):
        self.peers(1, lambda p: self.s2_copy(p, p).wait_recv(), near=True)
        total = self.r2[0].astype(F32)
        for p in range(1, self.second):
            total = total + self.r2[p].astype(F32)
        return self.special(total).astype(BF16)

    def finish(self):
        self.peers(0, lambda p: self.s1_copy(p, self.pos[0]).wait_send())
        self.peers(1, lambda p: self.s2_copy(p, self.pos[1]).wait_send())


def kernel(area_ref, emb_hbm, w_hbm, obs_hbm, d_ref, red, *scratch):
    (emb, halo, w_ref, obs_raw, obs, wp, fbuf, pown, ps, pr, send_a, recv_a, vals, send_b, recv_b, hr, gf, gcat,
     mid_sum, send_c, recv_c, dw0, dw1) = scratch[:23]
    s3, r3, waits = scratch[23:26]
    bufs = (scratch[26:30], scratch[30:34])
    (load, h_send, h_recv, e_sem, a_send, a_recv, b_send, b_recv, g_send, g_recv, c_sem,
     s3_send, s3_recv, t_send, t_recv, tc_send, tc_recv) = scratch[34:51]
    sums = (scratch[51:55], scratch[55:59])

    me = lax.axis_index("ens")
    row = lax.axis_index("space")
    x_lo, y = over(me, RING), mod(me, RING)
    core = mod(row, 2)
    z = mod(over(row, 2), RING)
    x_hi = over(row, 2 * RING)
    x = 2 * x_hi + x_lo
    twin = (me, row + 1 - 2 * core)
    next_row = mod(row + 2 * core - 1 + NLAT, NLAT)
    other = (me, next_row)
    inner = (row > 0) & (row < NLAT - 1)

    order = [3 * mod(2 * (1 - core) + i * (1 + core), 3) for i in range(3)]
    w_loads = [pltpu.make_async_copy(w_hbm.at[pl.ds(t, 3)], w_ref.at[pl.ds(t, 3)], load.at[i])
               for i, t in enumerate(order)]
    emb_load = pltpu.make_async_copy(emb_hbm, emb, load.at[3])
    obs_load = pltpu.make_async_copy(obs_hbm, obs_raw, load.at[4])
    for copy in (w_loads[0], emb_load, *w_loads[1:], obs_load):
        copy.start()

    def at(x_, y_, z_):
        return (mod(x_, 2) * RING + y_, (over(x_, 2) * RING + z_) * 2 + core)

    barrier = pltpu.get_barrier_semaphore()

    def greet(device):
        pl.semaphore_signal(barrier, inc=1, device_id=device, device_id_type=MESH)

    def member(j):
        return mod(x_lo + 1 - mod(j, 2), 2) * RING + mod(y + far(over(j, 2), RING), RING)

    def ring_a(p):
        return at(x, y + (1 - core) * (p - y), z + core * (p - z))

    def ring_b(p):
        return at(x, y + core * (p - y), z + (1 - core) * (p - z))

    def ring_x(p):
        return at(p, y, z)

    pos_a = y + core * (z - y)
    pos_b = z + core * (y - z)

    greet(other)
    greet(twin)

    @steps(0, MEMBERS - 1)
    def _(j):
        greet((member(j), row))

    @steps(0, RING - 1)
    def _(i):
        greet(at(x, y, mod(z + far(i, RING), RING)))

    greet(at(mod(x + 2, 4), y, z))
    greet(at(mod(x + 2, 4) + 1 - 2 * mod(x, 2), y, z))
    greetings = MEMBERS - 1 + RING - 1 + 4

    for t in range(9):
        wp[t, 96:, :] = jnp.zeros((LANES - 96, LATENT), BF16)
    fbuf[LON:LON + 16, :] = jnp.zeros((16, LANES), F32)
    obs[...] = jnp.zeros_like(obs)

    def pad(part):
        w_loads[part].wait()
        for i in range(3):
            wp[order[part] + i, 0:CH, :] = w_ref[order[part] + i]

    pad(0)
    emb_load.wait()

    latitude = math.pi * ((row.astype(F32) + 0.5) / NLAT - 0.5)
    east_west = 1.0 / (0.25 + jnp.cos(jnp.full((1, LANES), latitude, F32)))

    def product(first):
        mat = wp[pl.ds(first, 3)].reshape(3 * LANES, LATENT)
        out = lax.dot_general(emb[...], mat, (((1,), (1,)), ((), ())), preferred_element_type=F32)
        return (pltpu.roll(out[:, 0:LANES], 1, 0), out[:, LANES:2 * LANES],
                pltpu.roll(out[:, 2 * LANES:3 * LANES], LON - 1, 0))

    def h_copy(k):
        return remote(ps.at[0, k], pr.at[0, k], h_send.at[k], h_recv.at[k], other)

    h_twin = remote(ps.at[1], pr.at[1], h_send.at[MEMBERS], h_recv.at[MEMBERS], twin)

    for slot in range(2):
        lower = (1 - core) if slot == 0 else core
        west, mid, east = product(6 * lower)
        pad(slot + 1)
        fbuf[0:LON, :] = west + mid + east
        for k in range(MEMBERS):
            ps[slot, k] = fbuf[BLOCK * k:BLOCK * k + SLOT, :].astype(BF16)
        if slot == 1:
            h_twin.start()
            continue
        pl.semaphore_wait(barrier, greetings)

        @steps(0, MEMBERS)
        def _(j):
            h_copy(member(j)).start()

    west, mid, east = product(3)
    fbuf[0:LON, :] = mid + east_west * (west + east)
    for k in range(MEMBERS):
        pown[k] = fbuf[BLOCK * k:BLOCK * k + SLOT, :]

    def a_copy(k, slot):
        return remote(send_a.at[k], recv_a.at[slot], a_send.at[k], a_recv.at[slot], (k, row))

    def forecast(k):
        h_copy(k).wait_recv()
        total = pown[k] + pr[1, k].astype(F32)
        return (total + jnp.where(inner, pr[0, k].astype(F32), 0.0)).astype(BF16)

    h_twin.wait_recv()

    @steps(0, MEMBERS - 1)
    def _(j):
        k = member(j)
        send_a[k] = forecast(k)
        a_copy(k, me).start()

    vals[me] = forecast(me).astype(F32)

    e_copy = remote(emb, halo, e_sem.at[0], e_sem.at[1], twin)
    e_copy.start()

    obs_load.wait()
    for i in range(BLOCK):
        obs[i:i + 1, 0:CH] = obs_raw[i]

    @steps(0, MEMBERS - 1)
    def _(j):
        k = member(MEMBERS - 2 - j)
        a_copy(k, k).wait_recv()
        vals[k] = recv_a[k].astype(F32)

    area = area_ref[...]

    def score(j, loss):
        rows = pl.ds(pl.multiple_of(8 * j, 8), 8)
        f = [vals[i, rows, :] for i in range(MEMBERS)]
        o = obs[rows, :]
        grad, pair, total = [], [None] * MEMBERS, None
        pairs = None
        for i in range(MEMBERS):
            d = f[i] - o
            q = d * d + SMOOTHING
            r = lax.rsqrt(q)
            grad.append(d * r)
            total = q * r if total is None else total + q * r
        for i in range(MEMBERS):
            for k in range(i + 1, MEMBERS):
                d = f[i] - f[k]
                q = d * d + SMOOTHING
                r = lax.rsqrt(q)
                u = d * r
                pair[i] = u if pair[i] is None else pair[i] + u
                pair[k] = -u if pair[k] is None else pair[k] - u
                pairs = q * r if pairs is None else pairs + q * r
        for i in range(MEMBERS):
            vals[i, rows, :] = area * (grad[i] - PAIR_COEF * pair[i])
        crps = total - 0.5 * PAIR_COEF * (2.0 * pairs + MEMBERS * math.sqrt(SMOOTHING))
        lon = 8 * j + lax.broadcasted_iota(jnp.int32, (8, LANES), 0)
        ch = lax.broadcasted_iota(jnp.int32, (8, LANES), 1)
        return loss + jnp.where((lon < BLOCK) & (ch < CH), crps, 0.0)

    loss = lax.fori_loop(0, SLOT // 8, score, jnp.zeros((8, LANES), F32))

    def b_copy(k, slot):
        return remote(send_b.at[k], recv_b.at[slot], b_send.at[k], b_recv.at[slot], (k, row))

    @steps(0, MEMBERS - 1)
    def _(j):
        k = member(j)
        send_b[k] = vals[k].astype(BF16)
        b_copy(k, me).start()

    recv_b[me] = vals[me].astype(BF16)

    loss = jnp.sum(area * loss)
    sub = lax.broadcasted_iota(jnp.int32, (16, HALF), 0)
    lead = jnp.full((16, HALF), loss, F32).astype(BF16).astype(F32)
    tail = jnp.where(sub == 0, lead, jnp.where(sub == 1, loss - lead, 0.0))
    dw0[4 * CH:SUM_ROWS - 16, :] = jnp.zeros((SUM_ROWS - 16 - 4 * CH, HALF), F32)
    dw0[SUM_ROWS - 16:, :] = tail
    dw1[5 * CH:, :] = jnp.zeros((SUM_ROWS - 5 * CH, HALF), F32)
    for h in range(2):
        mid_sum[h, 3 * CH:, :] = jnp.zeros((MID_ROWS - 3 * CH, HALF), F32)

    def g_copy(k):
        return remote(recv_b.at[k], hr.at[0, k], g_send.at[k], g_recv.at[k], other)

    g_copy(me).start()

    @steps(0, MEMBERS - 1)
    def _(j):
        k = member(MEMBERS - 2 - j)
        b_copy(k, k).wait_recv()
        g_copy(k).start()

    g_twin = remote(recv_b, hr.at[1], g_send.at[MEMBERS], g_recv.at[MEMBERS], twin)
    g_twin.start()

    def gather(slot, columns, block):
        for k in range(MEMBERS):
            gf[slot, 8 + BLOCK * k:8 + BLOCK * k + SLOT, :] = block(k).astype(F32)
        gf[slot, 7:8, :] = gf[slot, LON + 7:LON + 8, :]
        gf[slot, LON + 8:LON + 9, :] = gf[slot, 8:9, :]
        for b, column in enumerate(columns):
            gcat[:, column * LANES:(column + 1) * LANES] = gf[slot, 9 - b:9 - b + LON, :].astype(BF16)

    def outer(column, latent):
        return lax.dot_general(gcat[:, column * LANES:(column + 3) * LANES], latent, (((0,), (0,)), ((), ())),
                               preferred_element_type=F32)

    def part(out, i, h):
        return out[LANES * i:LANES * i + CH, HALF * h:HALF * (h + 1)]

    flows = (
        Flow(SHAPES[0], (x, pos_a), (ring_x, ring_a), True, dw0, bufs[0], sums[0]),
        Flow(SHAPES[1], (pos_a, x), (ring_a, ring_x), False, dw1, bufs[1], sums[1]),
    )

    gather(0, (7, 6, 8), lambda k: recv_b[k])
    out = outer(6, emb[...])
    for i in range(3):
        for h in range(2):
            scale = 1.0 if i == 0 else east_west[:, 0:1]
            mid_sum[h, CH * i:CH * (i + 1), :] = part(out, i, h) * scale
    send_c[...] = mid_sum[1 - core].astype(BF16)
    c_copy = remote(send_c, recv_c, c_sem.at[0], c_sem.at[1], twin)
    c_copy.start()
    e_copy.wait_recv()
    with_twin = outer(6, halo[...])

    @steps(0, MEMBERS)
    def _(k):
        g_copy(k).wait_recv()

    gather(1, (0, 1, 2), lambda k: jnp.where(inner, hr[0, k].astype(F32), 0.0))
    across = outer(0, emb[...])
    for group, base in ((1, 0), (0, 3)):
        for n, (b, h) in enumerate(UNITS[group]):
            rows = slice(CH * (base + n), CH * (base + n + 1))
            (dw0, dw1)[group][rows, :] = part(with_twin, (1, 0, 2)[b], h) + part(across, b, h)
    flows[1].step1()
    c_copy.wait_recv()
    dw0[0:3 * CH, :] = (mid_sum[core] + recv_c[...].astype(F32))[0:3 * CH]
    flows[0].step1()

    g_twin.wait_recv()
    gather(2, (3, 4, 5), lambda k: hr[1, k])
    near = [wp[pl.ds(6 * first, 3)].reshape(3 * LANES, LATENT) for first in (1 - core, core)]
    plain = jnp.concatenate(near + [wp[4]], axis=0)
    scaled = jnp.concatenate([wp[3], wp[5]], axis=0)
    moved = jnp.dot(gcat[:, 0:7 * LANES], plain, preferred_element_type=F32)
    moved_ew = jnp.dot(gcat[:, 7 * LANES:], scaled, preferred_element_type=F32)
    d_ref[...] = (moved + east_west[:, 0:1] * moved_ew).astype(BF16)

    for flow in flows:
        flow.step2()
    for g, flow in enumerate(flows):
        s3[g] = flow.step3()

    def s3_copy(p, slot):
        return remote(s3, r3.at[slot], s3_send.at[p], s3_recv.at[slot], ring_b(p))

    @steps(0, RING - 1)
    def _(i):
        s3_copy(mod(pos_b + far(i, RING), RING), pos_b).start()

    r3[pos_b] = s3[...]

    c_copy.wait_send()
    e_copy.wait_send()
    h_twin.wait_send()
    g_twin.wait_send()

    @steps(0, MEMBERS)
    def _(k):
        h_copy(k).wait_send()
        g_copy(k).wait_send()

    @steps(0, MEMBERS - 1)
    def _(j):
        k = member(j)
        a_copy(k, me).wait_send()
        b_copy(k, me).wait_send()

    for flow in flows:
        flow.finish()

    @steps(0, RING - 1)
    def _(i):
        p = mod(pos_b + far(RING - 2 - i, RING), RING)
        s3_copy(p, p).wait_recv()

    total = r3[0].astype(F32)
    for p in range(1, RING):
        total = total + r3[p].astype(F32)
    red[core, x, pos_a, 0] = flows[0].special(total[0]).astype(BF16)
    red[core, x, pos_a, 1] = total[1].astype(BF16)

    def ta_copy(g, x_, i):
        block = red.at[core, x_, pos_a, g]
        return remote(block, block, t_send.at[g], t_recv.at[x_, pos_a, g], ring_a(mod(pos_a + far(i, RING), RING)))

    def tx_copy(g, slot, i):
        block = red.at[core, x, slot, g]
        return remote(block, block, t_send.at[2 + g], t_recv.at[x, slot, g], ring_x(mod(x + far(i, 4), 4)))

    def along_x(g, slot):
        for i in range(3):
            tx_copy(g, slot, i).start()

    def along_ring(g, x_):
        for i in range(RING - 1):
            ta_copy(g, x_, i).start()

    def landed(x_, slot, g):
        block = red.at[core, x_, slot, g]
        remote(block, block, t_send.at[0], t_recv.at[x_, slot, g], twin).wait_recv()

    def left(sem, blocks, like):
        part = like.at[pl.ds(0, blocks)]
        pltpu.make_async_copy(part, part, t_send.at[sem]).wait()

    def tc_copy(half, x_):
        block = red.at[half, x_]
        return remote(block, block, tc_send.at[x_], tc_recv.at[x_], twin)

    along_x(1, pos_a)
    along_ring(0, x)
    along_x(0, pos_a)
    along_ring(1, x)

    def from_ring(*offsets):
        for offset in offsets:
            slot = mod(pos_a + offset, RING)
            landed(x, slot, 0)
            along_x(0, slot)

    def from_x(*offsets):
        for offset in offsets:
            x_ = mod(x + offset, 4)
            landed(x_, pos_a, 1)
            along_ring(1, x_)

    from_ring(1, 7)
    from_x(1, 3)
    from_ring(2, 6)
    from_x(2)
    from_ring(3, 5, 4)

    @steps(1, RING)
    def _(i):
        landed(x, mod(pos_a + i, RING), 1)

    tc_copy(core, x).start()

    @steps(0, RING - 1)
    def _(i):
        s3_copy(mod(pos_b + far(i, RING), RING), pos_b).wait_send()

    for offset in (1, 3, 2):
        x_ = mod(x + offset, 4)
        landed(x_, pos_a, 0)

        @steps(1, RING)
        def _(i):
            for g in range(2):
                landed(x_, mod(pos_a + i, RING), g)

        tc_copy(core, x_).start()

    left(0, RING - 1, flows[0].s2)
    left(1, 4 * (RING - 1), waits)
    left(2, 3 * RING, waits)
    left(3, 3, flows[0].s2)

    @steps(0, 4)
    def _(x_):
        tc_copy(1 - core, x_).wait_recv()

    @steps(0, 4)
    def _(x_):
        tc_copy(core, x_).wait_send()


def unpack(d_ref, red, loss_hbm, d_hbm, dw_hbm, buf, out, loss_ref, sem):
    move = pltpu.make_async_copy(d_ref, d_hbm, sem.at[9])
    move.start()
    for h in range(2):
        for x_ in range(4):
            for a_ in range(RING):
                for g, block in enumerate((x_ * RING + a_, a_ * 4 + x_)):
                    buf[g, h, 16 * block:16 * (block + 1), :] = red[h, x_, a_, g].astype(F32)
    tails = jnp.concatenate([buf[0, h, SUM_ROWS - 16:SUM_ROWS - 14, 0:1] for h in range(2)], axis=0)
    loss_ref[...] = jnp.sum(tails, axis=0, keepdims=True) * (1.0 / TALLY)
    copies = [pltpu.make_async_copy(loss_ref, loss_hbm, sem.at[10])]
    copies[0].start()

    def unit(t, h, g, core, i):
        out[t, :, HALF * h:HALF * (h + 1)] = buf[g, core, CH * i:CH * (i + 1), :] * (1.0 / TALLY)

    def leave(t):
        copies.append(pltpu.make_async_copy(out.at[t], dw_hbm.at[t], sem.at[t]))
        copies[-1].start()

    for i, t in enumerate(MIDDLE):
        for h in range(2):
            unit(t, h, 0, h, i)
        leave(t)
    for core in range(2):
        for b in range(3):
            for h in range(2):
                group = 0 if (b, h) in UNITS[0] else 1
                unit(6 * (1 - core) + b, h, group, core, (3, 0)[group] + UNITS[group].index((b, h)))
            leave(6 * (1 - core) + b)
    for copy in copies:
        copy.wait()
    move.wait()


def per_device(member_embedding, weights, verifying_observed_grid, area_weight):
    emb = member_embedding[0, :, 0, :].T
    obs = jnp.transpose(verifying_observed_grid, (2, 1, 0))
    vmem = pl.BlockSpec(memory_space=pltpu.VMEM)
    hbm = pl.BlockSpec(memory_space=pltpu.HBM)
    dma = lambda *n: pltpu.SemaphoreType.DMA(n)
    blocks = lambda kind: pltpu.VMEM((MEMBERS, SLOT, LANES), kind)
    scratch = [
        pltpu.VMEM((LON, LATENT), BF16),
        pltpu.VMEM((LON, LATENT), BF16),
        pltpu.VMEM((9, CH, LATENT), BF16),
        pltpu.VMEM((BLOCK, 1, CH), F32),
        pltpu.VMEM((SLOT, LANES), F32),
        pltpu.VMEM((9, LANES, LATENT), BF16),
        pltpu.VMEM((LON + 16, LANES), F32),
        blocks(F32),
        pltpu.VMEM((2, MEMBERS, SLOT, LANES), BF16),
        pltpu.VMEM((2, MEMBERS, SLOT, LANES), BF16),
        blocks(BF16),
        blocks(BF16),
        blocks(F32),
        blocks(BF16),
        blocks(BF16),
        pltpu.VMEM((2, MEMBERS, SLOT, LANES), BF16),
        pltpu.VMEM((3, LON + 32, LANES), F32),
        pltpu.VMEM((LON, 9 * LANES), BF16),
        pltpu.VMEM((2, MID_ROWS, HALF), F32),
        pltpu.VMEM((MID_ROWS, HALF), BF16),
        pltpu.VMEM((MID_ROWS, HALF), BF16),
        pltpu.VMEM((SUM_ROWS, HALF), F32),
        pltpu.VMEM((SUM_ROWS, HALF), F32),
        pltpu.VMEM((2, 16, HALF), BF16),
        pltpu.VMEM((RING, 2, 16, HALF), BF16),
        pltpu.VMEM((4 * RING, 16, HALF), BF16),
    ]
    for first, second in SHAPES:
        big = pltpu.VMEM((first, 16 * second, HALF), BF16)
        small = pltpu.VMEM((second, 16, HALF), BF16)
        scratch += [big, big, small, small]
    scratch += [dma(5), dma(MEMBERS + 1), dma(MEMBERS + 1), dma(2),
                dma(MEMBERS), dma(MEMBERS), dma(MEMBERS), dma(MEMBERS), dma(MEMBERS + 1), dma(MEMBERS + 1), dma(2),
                dma(RING), dma(RING), dma(4), dma(4, RING, 2), dma(4), dma(4)]
    for first, second in SHAPES:
        for size in (first, second):
            scratch += [dma(size), dma(size)]
    moved, red = pl.pallas_call(
        kernel,
        out_shape=(jax.ShapeDtypeStruct((LON, LATENT), BF16),
                   jax.ShapeDtypeStruct((2, 4, RING, 2, 16, HALF), BF16)),
        in_specs=[vmem, hbm, hbm, hbm],
        out_specs=(vmem, vmem),
        scratch_shapes=scratch,
        compiler_params=pltpu.CompilerParams(
            collective_id=0, has_side_effects=True, vmem_limit_bytes=48 * 1024 * 1024),
        cost_estimate=pl.CostEstimate(flops=2_600_000_000, bytes_accessed=6_000_000, transcendentals=1_000_000),
        name="decoder",
    )(jnp.broadcast_to(area_weight, (8, LANES)), *(pltpu.with_memory_space_constraint(a, pltpu.HBM) for a in (emb, weights, obs)))
    loss, moved, grad_weight = pl.pallas_call(
        unpack,
        out_shape=(jax.ShapeDtypeStruct((1, 1), F32), jax.ShapeDtypeStruct((LON, LATENT), BF16),
                   jax.ShapeDtypeStruct((9, CH, LATENT), F32)),
        in_specs=[vmem, vmem],
        out_specs=(hbm, hbm, hbm),
        scratch_shapes=[pltpu.VMEM((2, 2, SUM_ROWS, HALF), F32), pltpu.VMEM((9, CH, LATENT), F32),
                        pltpu.VMEM((1, 1), F32), dma(11)],
        compiler_params=pltpu.CompilerParams(vmem_limit_bytes=32 * 1024 * 1024),
        cost_estimate=pl.CostEstimate(flops=1_000_000, bytes_accessed=4_500_000, transcendentals=0),
        name="unpack",
    )(moved, red)
    return loss.reshape(()), moved.T[None, :, None, :], grad_weight


def solution(mesh):
    return jax.shard_map(
        per_device,
        mesh=mesh,
        in_specs=(P("ens", None, "space", None), P(), P(None, "space", "ens"), P("space")),
        out_specs=(P(), P("ens", None, "space", None), P()),
        check_vma=False,
    )
```

```python
import math

import jax
import jax.numpy as jnp
from jax import lax
from jax.experimental import pallas as pl
from jax.experimental.pallas import tpu as pltpu
from jax.sharding import PartitionSpec as P

MESH = pl.DeviceIdType.MESH
F32 = jnp.float32
BF16 = jnp.bfloat16

CH, LATENT, LON, MEMBERS, NLAT = 100, 512, 720, 16, 32
LANES = 128
BLOCK = LON // MEMBERS
SLOT = 48
RING = 8
HALF = LATENT // 2
SUM_ROWS = 512
SMOOTHING = 0.01
PAIR_COEF = (1.0 - 0.05 / MEMBERS) / (MEMBERS - 1)
TALLY = MEMBERS * NLAT * LON
MIDDLE = (4, 3, 5)
UNITS = (((0, 0),), ((0, 1), (1, 0), (1, 1), (2, 0), (2, 1)))
MID_ROWS = 304
SHAPES = ((4, 8), (8, 4))


def steps(first, end):
    return pl.loop(first, end, unroll=True)


def remote(src, dst, send_sem, recv_sem, device):
    return pltpu.make_async_remote_copy(
        src_ref=src, dst_ref=dst, send_sem=send_sem, recv_sem=recv_sem,
        device_id=device, device_id_type=MESH,
    )


def mod(a, n):
    return a % n if isinstance(a, int) else lax.rem(a, jnp.int32(n))


def over(a, n):
    return a // n if isinstance(a, int) else lax.div(a, jnp.int32(n))


def far(i, size):
    odd = mod(i, 2)
    return size // 2 + over(i, 2) * (1 - odd) - over(i + 1, 2) * odd


def resplit(block):
    total = block[0:1] + block[1:2]
    lead = total.astype(BF16).astype(F32)
    row = lax.broadcasted_iota(jnp.int32, block.shape, 0)
    return jnp.where(row == 0, lead, jnp.where(row == 1, total - lead, block))


class Flow:
    def __init__(self, shape, pos, rings, has_loss, dw, bufs, sems):
        self.first, self.second = shape
        self.pos, self.rings = pos, rings
        self.has_loss = has_loss
        self.dw = dw
        self.s1, self.r1, self.s2, self.r2 = bufs
        self.sems = sems
        self.rows = 16 * self.second

    def copy(self, phase, src, dst, send, recv, device):
        return remote(src, dst, self.sems[2 * phase].at[send], self.sems[2 * phase + 1].at[recv], device)

    def s1_copy(self, p, slot):
        return self.copy(0, self.s1.at[p], self.r1.at[slot], p, slot, self.rings[0](p))

    def s2_copy(self, p, slot):
        return self.copy(1, self.s2.at[p], self.r2.at[slot], p, slot, self.rings[1](p))

    def peers(self, ring, body, near=False):
        size = (self.first, self.second)[ring]

        @steps(0, size - 1)
        def _(i):
            body(mod(self.pos[ring] + far(size - 2 - i if near else i, size), size))

    def step1(self):
        for p in range(self.first):
            self.s1[p] = self.dw[p * self.rows:(p + 1) * self.rows, :].astype(BF16)
        self.peers(0, lambda p: self.s1_copy(p, self.pos[0]).start())
        self.r1[self.pos[0]] = self.s1[self.pos[0]]

    def step2(self):
        self.peers(0, lambda p: self.s1_copy(p, p).wait_recv(), near=True)
        total = self.r1[0].astype(F32)
        for p in range(1, self.first):
            total = total + self.r1[p].astype(F32)
        for q in range(self.second):
            block = total[16 * q:16 * (q + 1)]
            if self.has_loss and q == self.second - 1:
                block = jnp.where(self.pos[0] == self.first - 1, resplit(block), block)
            self.s2[q] = block.astype(BF16)
        self.peers(1, lambda p: self.s2_copy(p, self.pos[1]).start())
        self.r2[self.pos[1]] = self.s2[self.pos[1]]

    def special(self, block):
        if not self.has_loss:
            return block
        here = (self.pos[0] == self.first - 1) & (self.pos[1] == self.second - 1)
        return jnp.where(here, resplit(block), block)

    def step3(self):
        self.peers(1, lambda p: self.s2_copy(p, p).wait_recv(), near=True)
        total = self.r2[0].astype(F32)
        for p in range(1, self.second):
            total = total + self.r2[p].astype(F32)
        return self.special(total).astype(BF16)

    def finish(self):
        self.peers(0, lambda p: self.s1_copy(p, self.pos[0]).wait_send())
        self.peers(1, lambda p: self.s2_copy(p, self.pos[1]).wait_send())


def kernel(area_ref, emb_hbm, w_hbm, obs_hbm, d_ref, red, *scratch):
    (emb, halo, w_ref, obs_raw, obs, wp, fbuf, pown, ps, pr, send_a, recv_a, vals, send_b, recv_b, hr, gf, gcat,
     mid_sum, send_c, recv_c, dw0, dw1) = scratch[:23]
    s3, r3, waits = scratch[23:26]
    bufs = (scratch[26:30], scratch[30:34])
    (load, h_send, h_recv, e_sem, a_send, a_recv, b_send, b_recv, g_send, g_recv, c_sem,
     s3_send, s3_recv, t_send, t_recv, tc_send, tc_recv) = scratch[34:51]
    sums = (scratch[51:55], scratch[55:59])

    me = lax.axis_index("ens")
    row = lax.axis_index("space")
    x_lo, y = over(me, RING), mod(me, RING)
    core = mod(row, 2)
    z = mod(over(row, 2), RING)
    x_hi = over(row, 2 * RING)
    x = 2 * x_hi + x_lo
    twin = (me, row + 1 - 2 * core)
    next_row = mod(row + 2 * core - 1 + NLAT, NLAT)
    other = (me, next_row)
    inner = (row > 0) & (row < NLAT - 1)

    order = [3 * mod(2 * (1 - core) + i * (1 + core), 3) for i in range(3)]
    w_loads = [pltpu.make_async_copy(w_hbm.at[pl.ds(t, 3)], w_ref.at[pl.ds(t, 3)], load.at[i])
               for i, t in enumerate(order)]
    emb_load = pltpu.make_async_copy(emb_hbm, emb, load.at[3])
    obs_load = pltpu.make_async_copy(obs_hbm, obs_raw, load.at[4])
    for copy in (w_loads[0], emb_load, *w_loads[1:], obs_load):
        copy.start()

    def at(x_, y_, z_):
        return (mod(x_, 2) * RING + y_, (over(x_, 2) * RING + z_) * 2 + core)

    barrier = pltpu.get_barrier_semaphore()

    def greet(device):
        pl.semaphore_signal(barrier, inc=1, device_id=device, device_id_type=MESH)

    def member(j):
        return mod(x_lo + 1 - mod(j, 2), 2) * RING + mod(y + far(over(j, 2), RING), RING)

    def ring_a(p):
        return at(x, y + (1 - core) * (p - y), z + core * (p - z))

    def ring_b(p):
        return at(x, y + core * (p - y), z + (1 - core) * (p - z))

    def ring_x(p):
        return at(p, y, z)

    pos_a = y + core * (z - y)
    pos_b = z + core * (y - z)

    greet(other)
    greet(twin)

    @steps(0, MEMBERS - 1)
    def _(j):
        greet((member(j), row))

    @steps(0, RING - 1)
    def _(i):
        greet(at(x, y, mod(z + far(i, RING), RING)))

    greet(at(mod(x + 2, 4), y, z))
    greet(at(mod(x + 2, 4) + 1 - 2 * mod(x, 2), y, z))
    greetings = MEMBERS - 1 + RING - 1 + 4

    for t in range(9):
        wp[t, 96:, :] = jnp.zeros((LANES - 96, LATENT), BF16)
    fbuf[LON:LON + 16, :] = jnp.zeros((16, LANES), F32)
    obs[...] = jnp.zeros_like(obs)

    def pad(part):
        w_loads[part].wait()
        for i in range(3):
            wp[order[part] + i, 0:CH, :] = w_ref[order[part] + i]

    pad(0)
    emb_load.wait()

    latitude = math.pi * ((row.astype(F32) + 0.5) / NLAT - 0.5)
    east_west = 1.0 / (0.25 + jnp.cos(jnp.full((1, LANES), latitude, F32)))

    def product(first):
        mat = wp[pl.ds(first, 3)].reshape(3 * LANES, LATENT)
        out = lax.dot_general(emb[...], mat, (((1,), (1,)), ((), ())), preferred_element_type=F32)
        return (pltpu.roll(out[:, 0:LANES], 1, 0), out[:, LANES:2 * LANES],
                pltpu.roll(out[:, 2 * LANES:3 * LANES], LON - 1, 0))

    def h_copy(k):
        return remote(ps.at[0, k], pr.at[0, k], h_send.at[k], h_recv.at[k], other)

    h_twin = remote(ps.at[1], pr.at[1], h_send.at[MEMBERS], h_recv.at[MEMBERS], twin)

    for slot in range(2):
        lower = (1 - core) if slot == 0 else core
        west, mid, east = product(6 * lower)
        pad(slot + 1)
        fbuf[0:LON, :] = west + mid + east
        for k in range(MEMBERS):
            ps[slot, k] = fbuf[BLOCK * k:BLOCK * k + SLOT, :].astype(BF16)
        if slot == 1:
            h_twin.start()
            continue
        pl.semaphore_wait(barrier, greetings)

        @steps(0, MEMBERS)
        def _(j):
            h_copy(member(j)).start()

    west, mid, east = product(3)
    fbuf[0:LON, :] = mid + east_west * (west + east)
    for k in range(MEMBERS):
        pown[k] = fbuf[BLOCK * k:BLOCK * k + SLOT, :]

    def a_copy(k, slot):
        return remote(send_a.at[k], recv_a.at[slot], a_send.at[k], a_recv.at[slot], (k, row))

    def forecast(k):
        h_copy(k).wait_recv()
        total = pown[k] + pr[1, k].astype(F32)
        return (total + jnp.where(inner, pr[0, k].astype(F32), 0.0)).astype(BF16)

    h_twin.wait_recv()

    @steps(0, MEMBERS - 1)
    def _(j):
        k = member(j)
        send_a[k] = forecast(k)
        a_copy(k, me).start()

    vals[me] = forecast(me).astype(F32)

    e_copy = remote(emb, halo, e_sem.at[0], e_sem.at[1], twin)
    e_copy.start()

    obs_load.wait()
    for i in range(BLOCK):
        obs[i:i + 1, 0:CH] = obs_raw[i]

    @steps(0, MEMBERS - 1)
    def _(j):
        k = member(MEMBERS - 2 - j)
        a_copy(k, k).wait_recv()
        vals[k] = recv_a[k].astype(F32)

    area = area_ref[...]

    def score(j, loss):
        rows = pl.ds(pl.multiple_of(8 * j, 8), 8)
        f = [vals[i, rows, :] for i in range(MEMBERS)]
        o = obs[rows, :]
        grad, pair, total = [], [None] * MEMBERS, None
        pairs = None
        for i in range(MEMBERS):
            d = f[i] - o
            q = d * d + SMOOTHING
            r = lax.rsqrt(q)
            grad.append(d * r)
            total = q * r if total is None else total + q * r
        for i in range(MEMBERS):
            for k in range(i + 1, MEMBERS):
                d = f[i] - f[k]
                q = d * d + SMOOTHING
                r = lax.rsqrt(q)
                u = d * r
                pair[i] = u if pair[i] is None else pair[i] + u
                pair[k] = -u if pair[k] is None else pair[k] - u
                pairs = q * r if pairs is None else pairs + q * r
        for i in range(MEMBERS):
            vals[i, rows, :] = area * (grad[i] - PAIR_COEF * pair[i])
        crps = total - 0.5 * PAIR_COEF * (2.0 * pairs + MEMBERS * math.sqrt(SMOOTHING))
        lon = 8 * j + lax.broadcasted_iota(jnp.int32, (8, LANES), 0)
        ch = lax.broadcasted_iota(jnp.int32, (8, LANES), 1)
        return loss + jnp.where((lon < BLOCK) & (ch < CH), crps, 0.0)

    loss = lax.fori_loop(0, SLOT // 8, score, jnp.zeros((8, LANES), F32))

    def b_copy(k, slot):
        return remote(send_b.at[k], recv_b.at[slot], b_send.at[k], b_recv.at[slot], (k, row))

    @steps(0, MEMBERS - 1)
    def _(j):
        k = member(j)
        send_b[k] = vals[k].astype(BF16)
        b_copy(k, me).start()

    recv_b[me] = vals[me].astype(BF16)

    loss = jnp.sum(area * loss)
    sub = lax.broadcasted_iota(jnp.int32, (16, HALF), 0)
    lead = jnp.full((16, HALF), loss, F32).astype(BF16).astype(F32)
    tail = jnp.where(sub == 0, lead, jnp.where(sub == 1, loss - lead, 0.0))
    dw0[4 * CH:SUM_ROWS - 16, :] = jnp.zeros((SUM_ROWS - 16 - 4 * CH, HALF), F32)
    dw0[SUM_ROWS - 16:, :] = tail
    dw1[5 * CH:, :] = jnp.zeros((SUM_ROWS - 5 * CH, HALF), F32)
    for h in range(2):
        mid_sum[h, 3 * CH:, :] = jnp.zeros((MID_ROWS - 3 * CH, HALF), F32)

    def g_copy(k):
        return remote(recv_b.at[k], hr.at[0, k], g_send.at[k], g_recv.at[k], other)

    g_copy(me).start()

    @steps(0, MEMBERS - 1)
    def _(j):
        k = member(MEMBERS - 2 - j)
        b_copy(k, k).wait_recv()
        g_copy(k).start()

    g_twin = remote(recv_b, hr.at[1], g_send.at[MEMBERS], g_recv.at[MEMBERS], twin)
    g_twin.start()

    def gather(slot, columns, block):
        for k in range(MEMBERS):
            gf[slot, 8 + BLOCK * k:8 + BLOCK * k + SLOT, :] = block(k).astype(F32)
        gf[slot, 7:8, :] = gf[slot, LON + 7:LON + 8, :]
        gf[slot, LON + 8:LON + 9, :] = gf[slot, 8:9, :]
        for b, column in enumerate(columns):
            gcat[:, column * LANES:(column + 1) * LANES] = gf[slot, 9 - b:9 - b + LON, :].astype(BF16)

    def outer(column, latent):
        return lax.dot_general(gcat[:, column * LANES:(column + 3) * LANES], latent, (((0,), (0,)), ((), ())),
                               preferred_element_type=F32)

    def part(out, i, h):
        return out[LANES * i:LANES * i + CH, HALF * h:HALF * (h + 1)]

    flows = (
        Flow(SHAPES[0], (x, pos_a), (ring_x, ring_a), True, dw0, bufs[0], sums[0]),
        Flow(SHAPES[1], (pos_a, x), (ring_a, ring_x), False, dw1, bufs[1], sums[1]),
    )

    gather(0, (7, 6, 8), lambda k: recv_b[k])
    out = outer(6, emb[...])
    for i in range(3):
        for h in range(2):
            scale = 1.0 if i == 0 else east_west[:, 0:1]
            mid_sum[h, CH * i:CH * (i + 1), :] = part(out, i, h) * scale
    send_c[...] = mid_sum[1 - core].astype(BF16)
    c_copy = remote(send_c, recv_c, c_sem.at[0], c_sem.at[1], twin)
    c_copy.start()
    e_copy.wait_recv()
    with_twin = outer(6, halo[...])

    @steps(0, MEMBERS)
    def _(k):
        g_copy(k).wait_recv()

    gather(1, (0, 1, 2), lambda k: jnp.where(inner, hr[0, k].astype(F32), 0.0))
    across = outer(0, emb[...])
    for group, base in ((1, 0), (0, 3)):
        for n, (b, h) in enumerate(UNITS[group]):
            rows = slice(CH * (base + n), CH * (base + n + 1))
            (dw0, dw1)[group][rows, :] = part(with_twin, (1, 0, 2)[b], h) + part(across, b, h)
    flows[1].step1()
    c_copy.wait_recv()
    dw0[0:3 * CH, :] = (mid_sum[core] + recv_c[...].astype(F32))[0:3 * CH]
    flows[0].step1()

    g_twin.wait_recv()
    gather(2, (3, 4, 5), lambda k: hr[1, k])
    near = [wp[pl.ds(6 * first, 3)].reshape(3 * LANES, LATENT) for first in (1 - core, core)]
    plain = jnp.concatenate(near + [wp[4]], axis=0)
    scaled = jnp.concatenate([wp[3], wp[5]], axis=0)
    moved = jnp.dot(gcat[:, 0:7 * LANES], plain, preferred_element_type=F32)
    moved_ew = jnp.dot(gcat[:, 7 * LANES:], scaled, preferred_element_type=F32)
    d_ref[...] = (moved + east_west[:, 0:1] * moved_ew).astype(BF16)

    for flow in flows:
        flow.step2()
    for g, flow in enumerate(flows):
        s3[g] = flow.step3()

    def s3_copy(p, slot):
        return remote(s3, r3.at[slot], s3_send.at[p], s3_recv.at[slot], ring_b(p))

    @steps(0, RING - 1)
    def _(i):
        s3_copy(mod(pos_b + far(i, RING), RING), pos_b).start()

    r3[pos_b] = s3[...]

    c_copy.wait_send()
    e_copy.wait_send()
    h_twin.wait_send()
    g_twin.wait_send()

    @steps(0, MEMBERS)
    def _(k):
        h_copy(k).wait_send()
        g_copy(k).wait_send()

    @steps(0, MEMBERS - 1)
    def _(j):
        k = member(j)
        a_copy(k, me).wait_send()
        b_copy(k, me).wait_send()

    for flow in flows:
        flow.finish()

    @steps(0, RING - 1)
    def _(i):
        p = mod(pos_b + far(RING - 2 - i, RING), RING)
        s3_copy(p, p).wait_recv()

    total = r3[0].astype(F32)
    for p in range(1, RING):
        total = total + r3[p].astype(F32)
    red[core, x, pos_a, 0] = flows[0].special(total[0]).astype(BF16)
    red[core, x, pos_a, 1] = total[1].astype(BF16)

    def along_x(block, send, recv):
        for i in range(3):
            remote(block, block, t_send.at[send], recv, ring_x(mod(x + far(i, 4), 4))).start()

    def along_ring(block, send, recv):
        for i in range(RING - 1):
            remote(block, block, t_send.at[send], recv, ring_a(mod(pos_a + far(i, RING), RING))).start()

    def landed(block, recv):
        remote(block, block, t_send.at[0], recv, twin).wait_recv()

    def left(sem, blocks, like):
        part = like.at[pl.ds(0, blocks)]
        pltpu.make_async_copy(part, part, t_send.at[sem]).wait()

    def tc_copy(half, x_):
        block = red.at[half, x_]
        return remote(block, block, tc_send.at[x_], tc_recv.at[x_], twin)

    along_x(red.at[core, x, pos_a], 3, t_recv.at[x, pos_a, 0])
    along_ring(red.at[core, x, pos_a], 0, t_recv.at[x, pos_a, 0])

    def from_ring(*offsets):
        for offset in offsets:
            slot = mod(pos_a + offset, RING)
            landed(red.at[core, x, slot], t_recv.at[x, slot, 0])
            along_x(red.at[core, x, slot, 0], 2, t_recv.at[x, slot, 0])

    def from_x(*offsets):
        for offset in offsets:
            x_ = mod(x + offset, 4)
            landed(red.at[core, x_, pos_a], t_recv.at[x_, pos_a, 0])
            along_ring(red.at[core, x_, pos_a, 1], 1, t_recv.at[x_, pos_a, 1])

    from_ring(1, 7)
    from_x(1, 3)
    from_ring(2, 6)
    from_x(2)
    from_ring(3, 5, 4)

    tc_copy(core, x).start()

    @steps(0, RING - 1)
    def _(i):
        s3_copy(mod(pos_b + far(i, RING), RING), pos_b).wait_send()

    for offset in (1, 3, 2):
        x_ = mod(x + offset, 4)

        @steps(1, RING)
        def _(i):
            slot = mod(pos_a + i, RING)
            for g in range(2):
                landed(red.at[core, x_, slot, g], t_recv.at[x_, slot, g])

        tc_copy(core, x_).start()

    left(0, 2 * (RING - 1), waits)
    left(1, 3 * (RING - 1), waits)
    left(2, 3 * (RING - 1), waits)
    left(3, 2 * 3, waits)

    @steps(0, 4)
    def _(x_):
        tc_copy(1 - core, x_).wait_recv()

    @steps(0, 4)
    def _(x_):
        tc_copy(core, x_).wait_send()


def unpack(d_ref, red, loss_hbm, d_hbm, dw_hbm, buf, out, loss_ref, sem):
    move = pltpu.make_async_copy(d_ref, d_hbm, sem.at[9])
    move.start()
    for h in range(2):
        for x_ in range(4):
            for a_ in range(RING):
                for g, block in enumerate((x_ * RING + a_, a_ * 4 + x_)):
                    buf[g, h, 16 * block:16 * (block + 1), :] = red[h, x_, a_, g].astype(F32)
    tails = jnp.concatenate([buf[0, h, SUM_ROWS - 16:SUM_ROWS - 14, 0:1] for h in range(2)], axis=0)
    loss_ref[...] = jnp.sum(tails, axis=0, keepdims=True) * (1.0 / TALLY)
    copies = [pltpu.make_async_copy(loss_ref, loss_hbm, sem.at[10])]
    copies[0].start()

    def unit(t, h, g, core, i):
        out[t, :, HALF * h:HALF * (h + 1)] = buf[g, core, CH * i:CH * (i + 1), :] * (1.0 / TALLY)

    def leave(t):
        copies.append(pltpu.make_async_copy(out.at[t], dw_hbm.at[t], sem.at[t]))
        copies[-1].start()

    for i, t in enumerate(MIDDLE):
        for h in range(2):
            unit(t, h, 0, h, i)
        leave(t)
    for core in range(2):
        for b in range(3):
            for h in range(2):
                group = 0 if (b, h) in UNITS[0] else 1
                unit(6 * (1 - core) + b, h, group, core, (3, 0)[group] + UNITS[group].index((b, h)))
            leave(6 * (1 - core) + b)
    for copy in copies:
        copy.wait()
    move.wait()


def per_device(member_embedding, weights, verifying_observed_grid, area_weight):
    emb = member_embedding[0, :, 0, :].T
    obs = jnp.transpose(verifying_observed_grid, (2, 1, 0))
    vmem = pl.BlockSpec(memory_space=pltpu.VMEM)
    hbm = pl.BlockSpec(memory_space=pltpu.HBM)
    dma = lambda *n: pltpu.SemaphoreType.DMA(n)
    blocks = lambda kind: pltpu.VMEM((MEMBERS, SLOT, LANES), kind)
    scratch = [
        pltpu.VMEM((LON, LATENT), BF16),
        pltpu.VMEM((LON, LATENT), BF16),
        pltpu.VMEM((9, CH, LATENT), BF16),
        pltpu.VMEM((BLOCK, 1, CH), F32),
        pltpu.VMEM((SLOT, LANES), F32),
        pltpu.VMEM((9, LANES, LATENT), BF16),
        pltpu.VMEM((LON + 16, LANES), F32),
        blocks(F32),
        pltpu.VMEM((2, MEMBERS, SLOT, LANES), BF16),
        pltpu.VMEM((2, MEMBERS, SLOT, LANES), BF16),
        blocks(BF16),
        blocks(BF16),
        blocks(F32),
        blocks(BF16),
        blocks(BF16),
        pltpu.VMEM((2, MEMBERS, SLOT, LANES), BF16),
        pltpu.VMEM((3, LON + 32, LANES), F32),
        pltpu.VMEM((LON, 9 * LANES), BF16),
        pltpu.VMEM((2, MID_ROWS, HALF), F32),
        pltpu.VMEM((MID_ROWS, HALF), BF16),
        pltpu.VMEM((MID_ROWS, HALF), BF16),
        pltpu.VMEM((SUM_ROWS, HALF), F32),
        pltpu.VMEM((SUM_ROWS, HALF), F32),
        pltpu.VMEM((2, 16, HALF), BF16),
        pltpu.VMEM((RING, 2, 16, HALF), BF16),
        pltpu.VMEM((4 * RING, 16, HALF), BF16),
    ]
    for first, second in SHAPES:
        big = pltpu.VMEM((first, 16 * second, HALF), BF16)
        small = pltpu.VMEM((second, 16, HALF), BF16)
        scratch += [big, big, small, small]
    scratch += [dma(5), dma(MEMBERS + 1), dma(MEMBERS + 1), dma(2),
                dma(MEMBERS), dma(MEMBERS), dma(MEMBERS), dma(MEMBERS), dma(MEMBERS + 1), dma(MEMBERS + 1), dma(2),
                dma(RING), dma(RING), dma(4), dma(4, RING, 2), dma(4), dma(4)]
    for first, second in SHAPES:
        for size in (first, second):
            scratch += [dma(size), dma(size)]
    moved, red = pl.pallas_call(
        kernel,
        out_shape=(jax.ShapeDtypeStruct((LON, LATENT), BF16),
                   jax.ShapeDtypeStruct((2, 4, RING, 2, 16, HALF), BF16)),
        in_specs=[vmem, hbm, hbm, hbm],
        out_specs=(vmem, vmem),
        scratch_shapes=scratch,
        compiler_params=pltpu.CompilerParams(
            collective_id=0, has_side_effects=True, vmem_limit_bytes=48 * 1024 * 1024),
        cost_estimate=pl.CostEstimate(flops=2_600_000_000, bytes_accessed=6_000_000, transcendentals=1_000_000),
        name="decoder",
    )(jnp.broadcast_to(area_weight, (8, LANES)), *(pltpu.with_memory_space_constraint(a, pltpu.HBM) for a in (emb, weights, obs)))
    loss, moved, grad_weight = pl.pallas_call(
        unpack,
        out_shape=(jax.ShapeDtypeStruct((1, 1), F32), jax.ShapeDtypeStruct((LON, LATENT), BF16),
                   jax.ShapeDtypeStruct((9, CH, LATENT), F32)),
        in_specs=[vmem, vmem],
        out_specs=(hbm, hbm, hbm),
        scratch_shapes=[pltpu.VMEM((2, 2, SUM_ROWS, HALF), F32), pltpu.VMEM((9, CH, LATENT), F32),
                        pltpu.VMEM((1, 1), F32), dma(11)],
        compiler_params=pltpu.CompilerParams(vmem_limit_bytes=32 * 1024 * 1024),
        cost_estimate=pl.CostEstimate(flops=1_000_000, bytes_accessed=4_500_000, transcendentals=0),
        name="unpack",
    )(moved, red)
    return loss.reshape(()), moved.T[None, :, None, :], grad_weight


def solution(mesh):
    return jax.shard_map(
        per_device,
        mesh=mesh,
        in_specs=(P("ens", None, "space", None), P(), P(None, "space", "ens"), P("space")),
        out_specs=(P(), P("ens", None, "space", None), P()),
        check_vma=False,
    )
```

```python
import math

import jax
import jax.numpy as jnp
from jax import lax
from jax.experimental import pallas as pl
from jax.experimental.pallas import tpu as pltpu
from jax.sharding import PartitionSpec as P

MESH = pl.DeviceIdType.MESH
F32 = jnp.float32
BF16 = jnp.bfloat16

CH, LATENT, LON, MEMBERS, NLAT = 100, 512, 720, 16, 32
LANES = 128
BLOCK = LON // MEMBERS
SLOT = 48
RING = 8
HALF = LATENT // 2
SUM_ROWS = 512
SMOOTHING = 0.01
PAIR_COEF = (1.0 - 0.05 / MEMBERS) / (MEMBERS - 1)
TALLY = MEMBERS * NLAT * LON
MIDDLE = (4, 3, 5)
UNITS = (((0, 0),), ((0, 1), (1, 0), (1, 1), (2, 0), (2, 1)))
MID_ROWS = 304
SHAPES = ((4, 8), (8, 4))


def steps(first, end):
    return pl.loop(first, end, unroll=True)


def remote(src, dst, send_sem, recv_sem, device):
    return pltpu.make_async_remote_copy(
        src_ref=src, dst_ref=dst, send_sem=send_sem, recv_sem=recv_sem,
        device_id=device, device_id_type=MESH,
    )


def mod(a, n):
    return a % n if isinstance(a, int) else lax.rem(a, jnp.int32(n))


def over(a, n):
    return a // n if isinstance(a, int) else lax.div(a, jnp.int32(n))


def far(i, size):
    odd = mod(i, 2)
    return size // 2 + over(i, 2) * (1 - odd) - over(i + 1, 2) * odd


def resplit(block):
    total = block[0:1] + block[1:2]
    lead = total.astype(BF16).astype(F32)
    row = lax.broadcasted_iota(jnp.int32, block.shape, 0)
    return jnp.where(row == 0, lead, jnp.where(row == 1, total - lead, block))


class Flow:
    def __init__(self, shape, pos, rings, has_loss, dw, bufs, sems):
        self.first, self.second = shape
        self.pos, self.rings = pos, rings
        self.has_loss = has_loss
        self.dw = dw
        self.s1, self.r1, self.s2, self.r2 = bufs
        self.sems = sems
        self.rows = 16 * self.second

    def copy(self, phase, src, dst, send, recv, device):
        return remote(src, dst, self.sems[2 * phase].at[send], self.sems[2 * phase + 1].at[recv], device)

    def s1_copy(self, p, slot):
        return self.copy(0, self.s1.at[p], self.r1.at[slot], p, slot, self.rings[0](p))

    def s2_copy(self, p, slot):
        return self.copy(1, self.s2.at[p], self.r2.at[slot], p, slot, self.rings[1](p))

    def peers(self, ring, body, near=False):
        size = (self.first, self.second)[ring]

        @steps(0, size - 1)
        def _(i):
            body(mod(self.pos[ring] + far(size - 2 - i if near else i, size), size))

    def step1(self):
        for p in range(self.first):
            self.s1[p] = self.dw[p * self.rows:(p + 1) * self.rows, :].astype(BF16)
        self.peers(0, lambda p: self.s1_copy(p, self.pos[0]).start())
        self.r1[self.pos[0]] = self.s1[self.pos[0]]

    def step2(self):
        self.peers(0, lambda p: self.s1_copy(p, p).wait_recv(), near=True)
        total = self.r1[0].astype(F32)
        for p in range(1, self.first):
            total = total + self.r1[p].astype(F32)
        for q in range(self.second):
            block = total[16 * q:16 * (q + 1)]
            if self.has_loss and q == self.second - 1:
                block = jnp.where(self.pos[0] == self.first - 1, resplit(block), block)
            self.s2[q] = block.astype(BF16)
        self.peers(1, lambda p: self.s2_copy(p, self.pos[1]).start())
        self.r2[self.pos[1]] = self.s2[self.pos[1]]

    def special(self, block):
        if not self.has_loss:
            return block
        here = (self.pos[0] == self.first - 1) & (self.pos[1] == self.second - 1)
        return jnp.where(here, resplit(block), block)

    def step3(self):
        self.peers(1, lambda p: self.s2_copy(p, p).wait_recv(), near=True)
        total = self.r2[0].astype(F32)
        for p in range(1, self.second):
            total = total + self.r2[p].astype(F32)
        return self.special(total).astype(BF16)

    def finish(self):
        self.peers(0, lambda p: self.s1_copy(p, self.pos[0]).wait_send())
        self.peers(1, lambda p: self.s2_copy(p, self.pos[1]).wait_send())


def kernel(area_ref, emb_hbm, w_hbm, obs_hbm, d_ref, red, *scratch):
    (emb, halo, w_ref, obs_raw, obs, wp, fbuf, pown, ps, pr, send_a, recv_a, vals, send_b, recv_b, hr, gf, gcat,
     mid_sum, send_c, recv_c, dw0, dw1) = scratch[:23]
    s3, r3, waits = scratch[23:26]
    bufs = (scratch[26:30], scratch[30:34])
    (load, h_send, h_recv, e_sem, a_send, a_recv, b_send, b_recv, g_send, g_recv, c_sem,
     s3_send, s3_recv, t_send, t_recv, tc_send, tc_recv) = scratch[34:51]
    sums = (scratch[51:55], scratch[55:59])

    me = lax.axis_index("ens")
    row = lax.axis_index("space")
    x_lo, y = over(me, RING), mod(me, RING)
    core = mod(row, 2)
    z = mod(over(row, 2), RING)
    x_hi = over(row, 2 * RING)
    x = 2 * x_hi + x_lo
    twin = (me, row + 1 - 2 * core)
    next_row = mod(row + 2 * core - 1 + NLAT, NLAT)
    other = (me, next_row)
    inner = (row > 0) & (row < NLAT - 1)

    order = [3 * mod(2 * (1 - core) + i * (1 + core), 3) for i in range(3)]
    w_loads = [pltpu.make_async_copy(w_hbm.at[pl.ds(t, 3)], w_ref.at[pl.ds(t, 3)], load.at[i])
               for i, t in enumerate(order)]
    emb_load = pltpu.make_async_copy(emb_hbm, emb, load.at[3])
    obs_load = pltpu.make_async_copy(obs_hbm, obs_raw, load.at[4])
    for copy in (w_loads[0], emb_load, *w_loads[1:], obs_load):
        copy.start()

    def at(x_, y_, z_):
        return (mod(x_, 2) * RING + y_, (over(x_, 2) * RING + z_) * 2 + core)

    barrier = pltpu.get_barrier_semaphore()

    def greet(device):
        pl.semaphore_signal(barrier, inc=1, device_id=device, device_id_type=MESH)

    def member(j):
        return mod(x_lo + 1 - mod(j, 2), 2) * RING + mod(y + far(over(j, 2), RING), RING)

    def ring_a(p):
        return at(x, y + (1 - core) * (p - y), z + core * (p - z))

    def ring_b(p):
        return at(x, y + core * (p - y), z + (1 - core) * (p - z))

    def ring_x(p):
        return at(p, y, z)

    pos_a = y + core * (z - y)
    pos_b = z + core * (y - z)

    greet(other)
    greet(twin)

    @steps(0, MEMBERS - 1)
    def _(j):
        greet((member(j), row))

    @steps(0, RING - 1)
    def _(i):
        greet(at(x, y, mod(z + far(i, RING), RING)))

    greet(at(mod(x + 2, 4), y, z))
    greet(at(mod(x + 2, 4) + 1 - 2 * mod(x, 2), y, z))
    greetings = MEMBERS - 1 + RING - 1 + 4

    for t in range(9):
        wp[t, 96:, :] = jnp.zeros((LANES - 96, LATENT), BF16)
    fbuf[LON:LON + 16, :] = jnp.zeros((16, LANES), F32)
    obs[...] = jnp.zeros_like(obs)

    def pad(part):
        w_loads[part].wait()
        for i in range(3):
            wp[order[part] + i, 0:CH, :] = w_ref[order[part] + i]

    pad(0)
    emb_load.wait()

    latitude = math.pi * ((row.astype(F32) + 0.5) / NLAT - 0.5)
    east_west = 1.0 / (0.25 + jnp.cos(jnp.full((1, LANES), latitude, F32)))

    def product(first):
        mat = wp[pl.ds(first, 3)].reshape(3 * LANES, LATENT)
        out = lax.dot_general(emb[...], mat, (((1,), (1,)), ((), ())), preferred_element_type=F32)
        return (pltpu.roll(out[:, 0:LANES], 1, 0), out[:, LANES:2 * LANES],
                pltpu.roll(out[:, 2 * LANES:3 * LANES], LON - 1, 0))

    def h_copy(k):
        return remote(ps.at[0, k], pr.at[0, k], h_send.at[k], h_recv.at[k], other)

    h_twin = remote(ps.at[1], pr.at[1], h_send.at[MEMBERS], h_recv.at[MEMBERS], twin)

    for slot in range(2):
        lower = (1 - core) if slot == 0 else core
        west, mid, east = product(6 * lower)
        pad(slot + 1)
        fbuf[0:LON, :] = west + mid + east
        for k in range(MEMBERS):
            ps[slot, k] = fbuf[BLOCK * k:BLOCK * k + SLOT, :].astype(BF16)
        if slot == 1:
            h_twin.start()
            continue
        pl.semaphore_wait(barrier, greetings)

        @steps(0, MEMBERS)
        def _(j):
            h_copy(member(j)).start()

    west, mid, east = product(3)
    fbuf[0:LON, :] = mid + east_west * (west + east)
    for k in range(MEMBERS):
        pown[k] = fbuf[BLOCK * k:BLOCK * k + SLOT, :]

    def a_copy(k, slot):
        return remote(send_a.at[k], recv_a.at[slot], a_send.at[k], a_recv.at[slot], (k, row))

    def forecast(k):
        h_copy(k).wait_recv()
        total = pown[k] + pr[1, k].astype(F32)
        return (total + jnp.where(inner, pr[0, k].astype(F32), 0.0)).astype(BF16)

    h_twin.wait_recv()

    @steps(0, MEMBERS - 1)
    def _(j):
        k = member(j)
        send_a[k] = forecast(k)
        a_copy(k, me).start()

    vals[me] = forecast(me).astype(F32)

    e_copy = remote(emb, halo, e_sem.at[0], e_sem.at[1], twin)
    e_copy.start()

    obs_load.wait()
    for i in range(BLOCK):
        obs[i:i + 1, 0:CH] = obs_raw[i]

    @steps(0, MEMBERS - 1)
    def _(j):
        k = member(MEMBERS - 2 - j)
        a_copy(k, k).wait_recv()
        vals[k] = recv_a[k].astype(F32)

    area = area_ref[...]

    def score(j, loss):
        rows = pl.ds(pl.multiple_of(8 * j, 8), 8)
        f = [vals[i, rows, :] for i in range(MEMBERS)]
        o = obs[rows, :]
        grad, pair, total = [], [None] * MEMBERS, None
        pairs = None
        for i in range(MEMBERS):
            d = f[i] - o
            q = d * d + SMOOTHING
            r = lax.rsqrt(q)
            grad.append(d * r)
            total = q * r if total is None else total + q * r
        for i in range(MEMBERS):
            for k in range(i + 1, MEMBERS):
                d = f[i] - f[k]
                q = d * d + SMOOTHING
                r = lax.rsqrt(q)
                u = d * r
                pair[i] = u if pair[i] is None else pair[i] + u
                pair[k] = -u if pair[k] is None else pair[k] - u
                pairs = q * r if pairs is None else pairs + q * r
        for i in range(MEMBERS):
            vals[i, rows, :] = area * (grad[i] - PAIR_COEF * pair[i])
        crps = total - 0.5 * PAIR_COEF * (2.0 * pairs + MEMBERS * math.sqrt(SMOOTHING))
        lon = 8 * j + lax.broadcasted_iota(jnp.int32, (8, LANES), 0)
        ch = lax.broadcasted_iota(jnp.int32, (8, LANES), 1)
        return loss + jnp.where((lon < BLOCK) & (ch < CH), crps, 0.0)

    loss = lax.fori_loop(0, SLOT // 8, score, jnp.zeros((8, LANES), F32))

    def b_copy(k, slot):
        return remote(send_b.at[k], recv_b.at[slot], b_send.at[k], b_recv.at[slot], (k, row))

    @steps(0, MEMBERS - 1)
    def _(j):
        k = member(j)
        send_b[k] = vals[k].astype(BF16)
        b_copy(k, me).start()

    recv_b[me] = vals[me].astype(BF16)

    loss = jnp.sum(area * loss)
    sub = lax.broadcasted_iota(jnp.int32, (16, HALF), 0)
    lead = jnp.full((16, HALF), loss, F32).astype(BF16).astype(F32)
    tail = jnp.where(sub == 0, lead, jnp.where(sub == 1, loss - lead, 0.0))
    dw0[4 * CH:SUM_ROWS - 16, :] = jnp.zeros((SUM_ROWS - 16 - 4 * CH, HALF), F32)
    dw0[SUM_ROWS - 16:, :] = tail
    dw1[5 * CH:, :] = jnp.zeros((SUM_ROWS - 5 * CH, HALF), F32)
    for h in range(2):
        mid_sum[h, 3 * CH:, :] = jnp.zeros((MID_ROWS - 3 * CH, HALF), F32)

    def g_copy(k):
        return remote(recv_b.at[k], hr.at[0, k], g_send.at[k], g_recv.at[k], other)

    g_copy(me).start()

    @steps(0, MEMBERS - 1)
    def _(j):
        k = member(MEMBERS - 2 - j)
        b_copy(k, k).wait_recv()
        g_copy(k).start()

    g_twin = remote(recv_b, hr.at[1], g_send.at[MEMBERS], g_recv.at[MEMBERS], twin)
    g_twin.start()

    def gather(slot, columns, block):
        for k in range(MEMBERS):
            gf[slot, 8 + BLOCK * k:8 + BLOCK * k + SLOT, :] = block(k).astype(F32)
        gf[slot, 7:8, :] = gf[slot, LON + 7:LON + 8, :]
        gf[slot, LON + 8:LON + 9, :] = gf[slot, 8:9, :]
        for b, column in enumerate(columns):
            gcat[:, column * LANES:(column + 1) * LANES] = gf[slot, 9 - b:9 - b + LON, :].astype(BF16)

    def outer(column, latent):
        return lax.dot_general(gcat[:, column * LANES:(column + 3) * LANES], latent, (((0,), (0,)), ((), ())),
                               preferred_element_type=F32)

    def part(out, i, h):
        return out[LANES * i:LANES * i + CH, HALF * h:HALF * (h + 1)]

    flows = (
        Flow(SHAPES[0], (x, pos_a), (ring_x, ring_a), True, dw0, bufs[0], sums[0]),
        Flow(SHAPES[1], (pos_a, x), (ring_a, ring_x), False, dw1, bufs[1], sums[1]),
    )

    gather(0, (7, 6, 8), lambda k: recv_b[k])
    out = outer(6, emb[...])
    for i in range(3):
        for h in range(2):
            scale = 1.0 if i == 0 else east_west[:, 0:1]
            mid_sum[h, CH * i:CH * (i + 1), :] = part(out, i, h) * scale
    send_c[...] = mid_sum[1 - core].astype(BF16)
    c_copy = remote(send_c, recv_c, c_sem.at[0], c_sem.at[1], twin)
    c_copy.start()
    e_copy.wait_recv()
    with_twin = outer(6, halo[...])

    @steps(0, MEMBERS)
    def _(k):
        g_copy(k).wait_recv()

    gather(1, (0, 1, 2), lambda k: jnp.where(inner, hr[0, k].astype(F32), 0.0))
    across = outer(0, emb[...])
    for group, base in ((1, 0), (0, 3)):
        for n, (b, h) in enumerate(UNITS[group]):
            rows = slice(CH * (base + n), CH * (base + n + 1))
            (dw0, dw1)[group][rows, :] = part(with_twin, (1, 0, 2)[b], h) + part(across, b, h)
    flows[1].step1()
    c_copy.wait_recv()
    dw0[0:3 * CH, :] = (mid_sum[core] + recv_c[...].astype(F32))[0:3 * CH]
    flows[0].step1()

    g_twin.wait_recv()
    gather(2, (3, 4, 5), lambda k: hr[1, k])
    near = [wp[pl.ds(6 * first, 3)].reshape(3 * LANES, LATENT) for first in (1 - core, core)]
    plain = jnp.concatenate(near + [wp[4]], axis=0)
    scaled = jnp.concatenate([wp[3], wp[5]], axis=0)
    moved = jnp.dot(gcat[:, 0:7 * LANES], plain, preferred_element_type=F32)
    moved_ew = jnp.dot(gcat[:, 7 * LANES:], scaled, preferred_element_type=F32)
    d_ref[...] = (moved + east_west[:, 0:1] * moved_ew).astype(BF16)

    for flow in flows:
        flow.step2()
    for g, flow in enumerate(flows):
        s3[g] = flow.step3()

    def s3_copy(p, slot):
        return remote(s3, r3.at[slot], s3_send.at[p], s3_recv.at[slot], ring_b(p))

    @steps(0, RING - 1)
    def _(i):
        s3_copy(mod(pos_b + far(i, RING), RING), pos_b).start()

    r3[pos_b] = s3[...]

    c_copy.wait_send()
    e_copy.wait_send()
    h_twin.wait_send()
    g_twin.wait_send()

    @steps(0, MEMBERS)
    def _(k):
        h_copy(k).wait_send()
        g_copy(k).wait_send()

    @steps(0, MEMBERS - 1)
    def _(j):
        k = member(j)
        a_copy(k, me).wait_send()
        b_copy(k, me).wait_send()

    for flow in flows:
        flow.finish()

    @steps(0, RING - 1)
    def _(i):
        p = mod(pos_b + far(RING - 2 - i, RING), RING)
        s3_copy(p, p).wait_recv()

    total = r3[0].astype(F32)
    for p in range(1, RING):
        total = total + r3[p].astype(F32)
    red[core, x, pos_a, 0] = flows[0].special(total[0]).astype(BF16)
    red[core, x, pos_a, 1] = total[1].astype(BF16)

    def ta_copy(g, x_, i):
        block = red.at[core, x_, pos_a, g]
        return remote(block, block, t_send.at[g], t_recv.at[x_, pos_a, g], ring_a(mod(pos_a + far(i, RING), RING)))

    def tx_copy(g, slot, i):
        block = red.at[core, x, slot, g]
        return remote(block, block, t_send.at[2 + g], t_recv.at[x, slot, g], ring_x(mod(x + far(i, 4), 4)))

    def along_x(g, slot):
        for i in range(3):
            tx_copy(g, slot, i).start()

    def along_ring(g, x_):
        for i in range(RING - 1):
            ta_copy(g, x_, i).start()

    def landed(x_, slot, g):
        block = red.at[core, x_, slot, g]
        remote(block, block, t_send.at[0], t_recv.at[x_, slot, g], twin).wait_recv()

    def left(sem, blocks, like):
        part = like.at[pl.ds(0, blocks)]
        pltpu.make_async_copy(part, part, t_send.at[sem]).wait()

    def tc_copy(half, x_):
        block = red.at[half, x_]
        return remote(block, block, tc_send.at[x_], tc_recv.at[x_], twin)

    along_x(1, pos_a)
    along_ring(0, x)
    along_x(0, pos_a)
    along_ring(1, x)

    def from_ring(*offsets):
        for offset in offsets:
            slot = mod(pos_a + offset, RING)
            landed(x, slot, 0)
            along_x(0, slot)

    def from_x(*offsets):
        for offset in offsets:
            x_ = mod(x + offset, 4)
            landed(x_, pos_a, 1)
            along_ring(1, x_)

    from_x(1, 3)
    from_ring(1, 7)
    from_x(2)
    from_ring(2, 6, 3, 5, 4)

    @steps(1, RING)
    def _(i):
        landed(x, mod(pos_a + i, RING), 1)

    tc_copy(core, x).start()

    @steps(0, RING - 1)
    def _(i):
        s3_copy(mod(pos_b + far(i, RING), RING), pos_b).wait_send()

    for offset in (1, 3, 2):
        x_ = mod(x + offset, 4)
        landed(x_, pos_a, 0)

        @steps(1, RING)
        def _(i):
            for g in range(2):
                landed(x_, mod(pos_a + i, RING), g)

        tc_copy(core, x_).start()

    left(0, RING - 1, flows[0].s2)
    left(1, 4 * (RING - 1), waits)
    left(2, 3 * RING, waits)
    left(3, 3, flows[0].s2)

    @steps(0, 4)
    def _(x_):
        tc_copy(1 - core, x_).wait_recv()

    @steps(0, 4)
    def _(x_):
        tc_copy(core, x_).wait_send()


def unpack(d_ref, red, loss_hbm, d_hbm, dw_hbm, buf, out, loss_ref, sem):
    move = pltpu.make_async_copy(d_ref, d_hbm, sem.at[9])
    move.start()
    for h in range(2):
        for x_ in range(4):
            for a_ in range(RING):
                for g, block in enumerate((x_ * RING + a_, a_ * 4 + x_)):
                    buf[g, h, 16 * block:16 * (block + 1), :] = red[h, x_, a_, g].astype(F32)
    tails = jnp.concatenate([buf[0, h, SUM_ROWS - 16:SUM_ROWS - 14, 0:1] for h in range(2)], axis=0)
    loss_ref[...] = jnp.sum(tails, axis=0, keepdims=True) * (1.0 / TALLY)
    copies = [pltpu.make_async_copy(loss_ref, loss_hbm, sem.at[10])]
    copies[0].start()

    def unit(t, h, g, core, i):
        out[t, :, HALF * h:HALF * (h + 1)] = buf[g, core, CH * i:CH * (i + 1), :] * (1.0 / TALLY)

    def leave(t):
        copies.append(pltpu.make_async_copy(out.at[t], dw_hbm.at[t], sem.at[t]))
        copies[-1].start()

    for i, t in enumerate(MIDDLE):
        for h in range(2):
            unit(t, h, 0, h, i)
        leave(t)
    for core in range(2):
        for b in range(3):
            for h in range(2):
                group = 0 if (b, h) in UNITS[0] else 1
                unit(6 * (1 - core) + b, h, group, core, (3, 0)[group] + UNITS[group].index((b, h)))
            leave(6 * (1 - core) + b)
    for copy in copies:
        copy.wait()
    move.wait()


def per_device(member_embedding, weights, verifying_observed_grid, area_weight):
    emb = member_embedding[0, :, 0, :].T
    obs = jnp.transpose(verifying_observed_grid, (2, 1, 0))
    vmem = pl.BlockSpec(memory_space=pltpu.VMEM)
    hbm = pl.BlockSpec(memory_space=pltpu.HBM)
    dma = lambda *n: pltpu.SemaphoreType.DMA(n)
    blocks = lambda kind: pltpu.VMEM((MEMBERS, SLOT, LANES), kind)
    scratch = [
        pltpu.VMEM((LON, LATENT), BF16),
        pltpu.VMEM((LON, LATENT), BF16),
        pltpu.VMEM((9, CH, LATENT), BF16),
        pltpu.VMEM((BLOCK, 1, CH), F32),
        pltpu.VMEM((SLOT, LANES), F32),
        pltpu.VMEM((9, LANES, LATENT), BF16),
        pltpu.VMEM((LON + 16, LANES), F32),
        blocks(F32),
        pltpu.VMEM((2, MEMBERS, SLOT, LANES), BF16),
        pltpu.VMEM((2, MEMBERS, SLOT, LANES), BF16),
        blocks(BF16),
        blocks(BF16),
        blocks(F32),
        blocks(BF16),
        blocks(BF16),
        pltpu.VMEM((2, MEMBERS, SLOT, LANES), BF16),
        pltpu.VMEM((3, LON + 32, LANES), F32),
        pltpu.VMEM((LON, 9 * LANES), BF16),
        pltpu.VMEM((2, MID_ROWS, HALF), F32),
        pltpu.VMEM((MID_ROWS, HALF), BF16),
        pltpu.VMEM((MID_ROWS, HALF), BF16),
        pltpu.VMEM((SUM_ROWS, HALF), F32),
        pltpu.VMEM((SUM_ROWS, HALF), F32),
        pltpu.VMEM((2, 16, HALF), BF16),
        pltpu.VMEM((RING, 2, 16, HALF), BF16),
        pltpu.VMEM((4 * RING, 16, HALF), BF16),
    ]
    for first, second in SHAPES:
        big = pltpu.VMEM((first, 16 * second, HALF), BF16)
        small = pltpu.VMEM((second, 16, HALF), BF16)
        scratch += [big, big, small, small]
    scratch += [dma(5), dma(MEMBERS + 1), dma(MEMBERS + 1), dma(2),
                dma(MEMBERS), dma(MEMBERS), dma(MEMBERS), dma(MEMBERS), dma(MEMBERS + 1), dma(MEMBERS + 1), dma(2),
                dma(RING), dma(RING), dma(4), dma(4, RING, 2), dma(4), dma(4)]
    for first, second in SHAPES:
        for size in (first, second):
            scratch += [dma(size), dma(size)]
    moved, red = pl.pallas_call(
        kernel,
        out_shape=(jax.ShapeDtypeStruct((LON, LATENT), BF16),
                   jax.ShapeDtypeStruct((2, 4, RING, 2, 16, HALF), BF16)),
        in_specs=[vmem, hbm, hbm, hbm],
        out_specs=(vmem, vmem),
        scratch_shapes=scratch,
        compiler_params=pltpu.CompilerParams(
            collective_id=0, has_side_effects=True, vmem_limit_bytes=48 * 1024 * 1024),
        cost_estimate=pl.CostEstimate(flops=2_600_000_000, bytes_accessed=6_000_000, transcendentals=1_000_000),
        name="decoder",
    )(jnp.broadcast_to(area_weight, (8, LANES)), *(pltpu.with_memory_space_constraint(a, pltpu.HBM) for a in (emb, weights, obs)))
    loss, moved, grad_weight = pl.pallas_call(
        unpack,
        out_shape=(jax.ShapeDtypeStruct((1, 1), F32), jax.ShapeDtypeStruct((LON, LATENT), BF16),
                   jax.ShapeDtypeStruct((9, CH, LATENT), F32)),
        in_specs=[vmem, vmem],
        out_specs=(hbm, hbm, hbm),
        scratch_shapes=[pltpu.VMEM((2, 2, SUM_ROWS, HALF), F32), pltpu.VMEM((9, CH, LATENT), F32),
                        pltpu.VMEM((1, 1), F32), dma(11)],
        compiler_params=pltpu.CompilerParams(vmem_limit_bytes=32 * 1024 * 1024),
        cost_estimate=pl.CostEstimate(flops=1_000_000, bytes_accessed=4_500_000, transcendentals=0),
        name="unpack",
    )(moved, red)
    return loss.reshape(()), moved.T[None, :, None, :], grad_weight


def solution(mesh):
    return jax.shard_map(
        per_device,
        mesh=mesh,
        in_specs=(P("ens", None, "space", None), P(), P(None, "space", "ens"), P("space")),
        out_specs=(P(), P("ens", None, "space", None), P()),
        check_vma=False,
    )
```
